512 devices in a mesh: fsdp: 128 (over y, z, core), tensor: 4 (over x).
Axes of the slice: x: 4, y: 4, z: 16, core: 2. Of those that a mesh axis runs over, the one named last changes fastest.
Arguments:
- gradients: bfloat16 [128, 1024, 1024], P(None, 'fsdp', 'tensor'), may hold values from -300 to 300
- parameters: bfloat16 [128, 1024, 1024], P(None, 'fsdp', 'tensor'), may hold values from -6 to 6
- left_root: bfloat16 [384, 1024, 1024], P('fsdp', 'tensor'), may hold values from -1 to 2
- right_root: bfloat16 [384, 1024, 1024], P('fsdp', None, 'tensor'), may hold values from -1 to 2
- assignment: int32 [128], replicated, may hold values from 0 to 383, as said below
Outputs:
- grafted_update: bfloat16 [128, 1024, 1024], P(None, 'fsdp', 'tensor')
- updated_params: bfloat16 [128, 1024, 1024], P(None, 'fsdp', 'tensor')
The draws below stay inside these ranges and needn't reach their ends.
Inputs may be any that keep to these rules, and one draw needn't show every extreme that they name: `assignment`: distinct slot numbers; slot s belongs to owner s // 3. Every draw fills all 3 slots of some owner, which one is drawn; owner loads are skewed and about half the owners get none.
All inputs are finite; a program needn't handle non-finite values.
Results may differ from the reference program's by a relative error of at most 0.0049.
Values may be sent and summed in bfloat16 or wider, within the bound.
No kernel may reach another device: no remote copies, remote signals or barrier semaphores. Data moves between devices by JAX's collectives and lax.ppermute only.
A program may use at most 64 MiB of HBM per device.

```python
import math
import jax
import jax.numpy as jnp
from jax import lax

FACTOR_ORDER = 1024
OWNER_SLOTS = 3
TOTAL_SLOTS = 384
NBLK = 128


def diagonal_part(key):
    ranked_values = jax.random.uniform(key, (TOTAL_SLOTS, 1, FACTOR_ORDER), minval=0.5, maxval=1.5)
    rows_iota = lax.broadcasted_iota(jnp.int32, (1, FACTOR_ORDER, FACTOR_ORDER), 1)
    cols_iota = lax.broadcasted_iota(jnp.int32, (1, FACTOR_ORDER, FACTOR_ORDER), 2)
    return jnp.where(rows_iota == cols_iota, ranked_values, 0.0)


def draw_left_root(key, part):
    key = jax.random.fold_in(key, 2)
    first, second_choice = jax.random.split(key)
    random_noise = jax.random.normal(second_choice, (TOTAL_SLOTS, FACTOR_ORDER, FACTOR_ORDER))
    return (diagonal_part(first) + random_noise * (0.6 / math.sqrt(FACTOR_ORDER))).astype(jnp.bfloat16)


def draw_right_root(key, part):
    key = jax.random.fold_in(key, 3)
    first, second_choice = jax.random.split(key)
    random_noise = jax.random.normal(second_choice, (TOTAL_SLOTS, FACTOR_ORDER, FACTOR_ORDER))
    return (diagonal_part(first) + random_noise * (0.6 / math.sqrt(FACTOR_ORDER))).astype(jnp.bfloat16)


def draw_gradients(key, part):
    key = jax.random.fold_in(key, 1)
    random_keys = jax.random.split(key, 4)
    position = jnp.arange(FACTOR_ORDER, dtype=jnp.float32)
    rising = jnp.exp(math.log(3.0) * position / (FACTOR_ORDER - 1))
    row_scale = rising[None, :] * jnp.exp(jax.random.uniform(random_keys[0], (NBLK, FACTOR_ORDER)) * math.log(10.0 / 3.0))
    col_scale = rising[None, :] * jnp.exp(jax.random.uniform(random_keys[1], (NBLK, FACTOR_ORDER)) * math.log(10.0 / 3.0))
    block_scale = jnp.exp(jax.random.uniform(random_keys[2], (NBLK, 1, 1), minval=-0.7, maxval=0.7))
    base = jax.random.normal(random_keys[3], (NBLK, FACTOR_ORDER, FACTOR_ORDER))
    ranked_values = base * row_scale[:, :, None] * col_scale[:, None, :] * block_scale * 0.1
    return jnp.clip(ranked_values, -300.0, 300.0).astype(jnp.bfloat16)


def draw_assignment(key, part):
    key = jax.random.fold_in(key, 7)
    random_keys = jax.random.split(key, 4)
    owner_devices = TOTAL_SLOTS // OWNER_SLOTS
    slot_holder_index = jnp.arange(TOTAL_SLOTS, dtype=jnp.int32) // OWNER_SLOTS
    heavy = jax.random.randint(random_keys[0], (), 0, owner_devices)
    owner_bias = jax.random.randint(random_keys[1], (owner_devices,), 0, 4)
    random_jitter = jax.random.randint(random_keys[2], (TOTAL_SLOTS,), 0, 1024)
    slot_priority = jnp.where(slot_holder_index == heavy, 8, owner_bias[slot_holder_index]) * 1024 + random_jitter
    slot_scores = slot_priority * TOTAL_SLOTS + jnp.arange(TOTAL_SLOTS, dtype=jnp.int32)
    unused, chosen = lax.top_k(slot_scores, NBLK)
    shuffle = jax.random.permutation(random_keys[3], NBLK)
    return chosen[shuffle].astype(jnp.int32)


def steps_of(own_key, dims, shards, smallest, top_value):
    gain, own = 1.0, jax.random.fold_in(own_key, 6)
    for axis_at, blocks in shards:
        steps = jnp.exp(jax.random.uniform(jax.random.fold_in(own, axis_at), (blocks,), jnp.float32, smallest / len(shards), top_value / len(shards)))
        gain = gain * jnp.repeat(steps, dims[axis_at] // blocks).reshape([-1 if axis == axis_at else 1 for axis in range(len(dims))])
    return gain


def noise(stream_key, extent, deviation, limit, shards=(), kind=jnp.bfloat16):
    level = steps_of(stream_key, extent, shards, -0.22, 0.18) if shards else 1.0
    values = jax.random.normal(stream_key, extent, jnp.float32) * deviation * level
    return jnp.minimum(jnp.maximum(values, -limit), limit).astype(kind)


def setup_inputs(seed: int = 0) -> dict:
    splits = jax.random.split(jax.random.key(seed), 6)
    gradients = draw_gradients(jax.random.fold_in(splits[5], 71), 0)
    parameters = noise(splits[1], (NBLK, FACTOR_ORDER, FACTOR_ORDER), 1.0, 6.0, ((1, 128), (2, 4)))
    left_root = draw_left_root(jax.random.fold_in(splits[5], 71), 0)
    right_root = draw_right_root(jax.random.fold_in(splits[5], 71), 0)
    assignment = draw_assignment(jax.random.fold_in(splits[5], 71), 0)
    return {"gradients": gradients, "parameters": parameters, "left_root": left_root, "right_root": right_root, "assignment": assignment}


graft_eps = 1e-06
step_rate = 0.1

def precondition_block(gradient, left_factor, right_factor):
    left_mixed = jnp.dot(left_factor, gradient, preferred_element_type=jnp.float32).astype(jnp.bfloat16)
    result = jnp.dot(left_mixed, right_factor, preferred_element_type=jnp.float32)
    grad_mean = jnp.mean(jnp.square(gradient.astype(jnp.float32)))
    update_mean = jnp.mean(jnp.square(result))
    factor = jnp.sqrt(grad_mean + graft_eps) / jnp.sqrt(update_mean + graft_eps)
    return (result * factor).astype(jnp.bfloat16)

def reference(gradients, parameters, left_root, right_root, assignment):

    def one_block(block_id):
        slot_id = assignment[block_id]
        return precondition_block(gradients[block_id], left_root[slot_id], right_root[slot_id])
    grafted = lax.map(one_block, jnp.arange(NBLK, dtype=jnp.int32))
    updated = (parameters.astype(jnp.float32) - step_rate * grafted.astype(jnp.float32)).astype(jnp.bfloat16)
    return (grafted, updated)
```

```python
import functools
import jax
import jax.numpy as jnp
from jax import lax
from jax.experimental import pallas as pl
from jax.experimental.pallas import tpu as pltpu
from jax.sharding import Mesh, PartitionSpec as P

graft_eps = 1e-06
step_rate = 0.1

grid_y, grid_z, grid_core, grid_x = 4, 16, 2, 4
plane_axes = ("y", "core", "x")
fsdp_axes = ("y", "z", "core")
plane_devices = grid_y * grid_core * grid_x
plane_capacities = (13, 15, 16, 18, 24)

pick_run = 8


def pick_kernel(index_ref, src_ref, out_ref):
    def some(step, carry):
        first = step * pick_run
        rows = [src_ref[index_ref[first + i]] for i in range(pick_run)]
        for i in range(pick_run):
            out_ref[first + i] = rows[i]
        return carry

    lax.fori_loop(0, out_ref.shape[0] // pick_run, some, 0)


def pick_runs_kernel(strides, index_ref, src_ref, out_ref):
    src_run, src_step, out_run, out_step = strides

    def one(at, carry):
        src_at, out_at = index_ref[at] * src_run, at * out_run
        for z in range(grid_z):
            out_ref[out_at + z * out_step] = src_ref[src_at + z * src_step]
        return carry

    lax.fori_loop(0, index_ref.shape[0], one, 0)


def step_kernel(step_ref, parameter_ref, new_ref):
    def some(at, carry):
        rows = pl.ds(at * pick_run, pick_run)
        new_ref[rows] = (
            parameter_ref[rows].astype(jnp.float32)
            - step_rate * step_ref[rows].astype(jnp.float32)
        ).astype(new_ref.dtype)
        return carry

    lax.fori_loop(0, new_ref.shape[0] // pick_run, some, 0)


def vmem_call(kernel, index, arrays, count, name):
    vmem_spec = pl.BlockSpec(memory_space=pltpu.VMEM)
    index_specs = [pl.BlockSpec(memory_space=pltpu.SMEM)] * len(index)
    return pl.pallas_call(
        kernel,
        out_shape=jax.ShapeDtypeStruct((count,) + arrays[0].shape[1:], arrays[0].dtype),
        in_specs=index_specs + [vmem_spec] * len(arrays),
        out_specs=vmem_spec,
        compiler_params=pltpu.CompilerParams(vmem_limit_bytes=32 * 1024 * 1024),
        name=name,
    )(*index, *arrays)


def place(values, keys, size):
    hit = jnp.arange(size, dtype=jnp.int32)[:, None] == keys[None, :]
    return jnp.sum(jnp.where(hit, values[None, :], 0), axis=1)


def holder_x(slot, core):
    return (slot + 2 + core) % grid_x


def slot_at(x, core):
    return (x + 2 * grid_x - 2 - core) % grid_x


def factor_pieces(factor, here, core):
    slots = factor.shape[0]
    got = []
    for shift in range(1, grid_x):
        slot = jnp.minimum(slot_at(here + shift, core), slots - 1)
        piece = lax.dynamic_index_in_dim(factor, slot, 0, keepdims=False)
        pairs = [
            (at * grid_x + src, at * grid_x + (src + shift) % grid_x)
            for at in range(grid_core)
            for src in range(grid_x)
            if slot_at((src + shift) % grid_x, at) < slots
        ]
        got.append(lax.ppermute(piece, ("core", "x"), pairs))
    return got


def slot_kernel(here_ref, *refs):
    rows = refs[0]
    lefts = refs[1 : 1 + grid_x]
    rights = refs[1 + grid_x : 1 + 2 * grid_x]
    out, left, right, block, mixed, product, sems = refs[1 + 2 * grid_x :]
    here, slot = here_ref[0], here_ref[1]
    order = block.shape[0]
    share = order // grid_x
    row_local = rows.shape[2]
    pair = grid_core * row_local
    tiles = order // pair
    copies = []
    for shift in range(grid_x):
        at = lax.rem(here - shift + grid_x, grid_x)
        left_src = lefts[0].at[slot] if shift == 0 else lefts[shift]
        right_src = rights[0].at[slot] if shift == 0 else rights[shift]
        copies.append(
            (
                pltpu.make_async_copy(left_src, left.at[at], sems.at[shift]),
                pltpu.make_async_copy(right_src, right.at[at], sems.at[grid_x + shift]),
            )
        )
    for copy, unused in copies:
        copy.start()
    for unused, copy in copies:
        copy.start()

    def gather_tile(tile, total):
        y, z = tile // grid_z, tile % grid_z
        at = pl.ds(pl.multiple_of(tile * pair, pair), pair)
        for x in range(grid_x):
            both = jnp.concatenate(
                [
                    rows[(y * grid_core + core) * grid_x + x, z].astype(jnp.float32)
                    for core in range(grid_core)
                ],
                axis=0,
            )
            total = total + both * both
            block[at, x * share : (x + 1) * share] = both.astype(block.dtype)
        return total

    grad_sum = lax.fori_loop(
        0, tiles, gather_tile, jnp.zeros((pair, share), jnp.float32)
    )
    for copy, unused in copies:
        copy.wait()

    def mix(tile, carry):
        at = pl.ds(pl.multiple_of(tile * share, share), share)
        for x in range(grid_x):
            mixed[x * share : (x + 1) * share, at] = jnp.dot(
                left[x], block[:, at], preferred_element_type=jnp.float32
            ).astype(mixed.dtype)
        return carry

    lax.fori_loop(0, grid_x, mix, 0)
    for unused, copy in copies:
        copy.wait()

    def finish(x, total):
        for tile in range(grid_x):
            at = slice(tile * share, (tile + 1) * share)
            part = jnp.dot(mixed[at, :], right[x], preferred_element_type=jnp.float32)
            product[x, at] = part
            total = total + jnp.sum(jnp.square(part), axis=0, keepdims=True)
        return total

    update_sum = lax.fori_loop(0, grid_x, finish, jnp.zeros((1, share), jnp.float32))
    entries = float(order * order)
    grad_ms = jnp.sum(grad_sum, axis=(0, 1), keepdims=True) / entries
    update_ms = jnp.sum(update_sum, axis=(0, 1), keepdims=True) / entries
    factor = jnp.sqrt(grad_ms + graft_eps) / jnp.sqrt(update_ms + graft_eps)

    def scatter_tile(tile, carry):
        y, z = tile // grid_z, tile % grid_z
        at = pl.ds(pl.multiple_of(tile * pair, pair), pair)
        for x in range(grid_x):
            scaled = (product[x, at, :] * factor).reshape(grid_core, row_local, share)
            for core in range(grid_core):
                out[(y * grid_core + core) * grid_x + x, z] = scaled[core].astype(out.dtype)
        return carry

    lax.fori_loop(0, tiles, scatter_tile, 0)


def precondition_slot(here, core, rows, left_root, right_root, left_pieces, right_pieces):
    slots, order = right_root.shape[:2]
    share = order // grid_x
    any_spec = pl.BlockSpec(memory_space=pl.ANY)
    vmem_spec = pl.BlockSpec(memory_space=pltpu.VMEM)
    return pl.pallas_call(
        slot_kernel,
        out_shape=jax.ShapeDtypeStruct(rows.shape, rows.dtype),
        in_specs=[pl.BlockSpec(memory_space=pltpu.SMEM)]
        + [vmem_spec]
        + [any_spec] * (2 * grid_x),
        out_specs=vmem_spec,
        scratch_shapes=[
            pltpu.VMEM((grid_x, share, order), jnp.bfloat16),
            pltpu.VMEM((grid_x, order, share), jnp.bfloat16),
            pltpu.VMEM((order, order), jnp.bfloat16),
            pltpu.VMEM((order, order), jnp.bfloat16),
            pltpu.VMEM((grid_x, order, share), jnp.float32),
            pltpu.SemaphoreType.DMA((2 * grid_x,)),
        ],
        compiler_params=pltpu.CompilerParams(vmem_limit_bytes=40 * 1024 * 1024),
        cost_estimate=pl.CostEstimate(
            flops=4 * order**3, bytes_accessed=8 * order * order, transcendentals=0
        ),
        name="precondition_slot",
    )(
        jnp.stack([here, jnp.minimum(slot_at(here, core), slots - 1)]),
        rows,
        left_root,
        *left_pieces,
        right_root,
        *right_pieces,
    )


def program(plane_cap, gradients, parameters, left_root, right_root, assignment):
    block_count, row_local, col_local = gradients.shape
    slots_each = left_root.shape[0]
    chunk = (row_local, col_local)
    here, core = lax.axis_index("x"), lax.axis_index("core")
    left_pieces = factor_pieces(left_root, here, core)
    right_pieces = factor_pieces(right_root, here, core)

    owner = assignment // slots_each
    plane = (owner // grid_core) % grid_z
    owner_core = owner % grid_core
    in_plane = ((owner // (grid_z * grid_core)) * grid_core + owner_core) * grid_x + holder_x(
        assignment % slots_each, owner_core
    )
    ids = jnp.arange(block_count, dtype=jnp.int32)
    earlier = (plane[:, None] == plane[None, :]) & (ids[None, :] < ids[:, None])
    rank = jnp.sum(earlier.astype(jnp.int32), axis=1)
    place_of = plane * plane_cap + rank
    my_z = lax.axis_index("z")
    block_at = place(ids, place_of, grid_z * plane_cap)
    mine = plane == my_z
    rank_at = place(rank, jnp.where(mine, in_plane, plane_devices), plane_devices)
    holder_at = place(in_plane, jnp.where(mine, rank, plane_cap), plane_cap)
    plane_rows, z_rows = plane_devices * grid_z, grid_z * plane_cap

    def z_hop(rows):
        rows = rows.reshape((grid_z, plane_cap) + chunk)
        return lax.all_to_all(rows, "z", 0, 0, tiled=True).reshape((z_rows,) + chunk)

    def plane_hop(rows):
        rows = rows.reshape((plane_devices, grid_z) + chunk)
        return lax.all_to_all(rows, plane_axes, 0, 0, tiled=True)

    rows = vmem_call(pick_kernel, [block_at], [gradients], z_rows, "pick_for_z")
    rows, left_pieces, right_pieces = lax.optimization_barrier(
        (z_hop(rows), left_pieces, right_pieces)
    )
    kernel = functools.partial(pick_runs_kernel, (1, plane_cap, grid_z, 1))
    rows = vmem_call(kernel, [rank_at], [rows], plane_rows, "pick_for_plane")
    rows = plane_hop(rows)
    update = precondition_slot(
        here, core, rows, left_root, right_root, left_pieces, right_pieces
    )
    update = plane_hop(update).reshape((plane_rows,) + chunk)
    kernel = functools.partial(pick_runs_kernel, (grid_z, 1, 1, plane_cap))
    update = vmem_call(kernel, [holder_at], [update], z_rows, "pick_back_for_z")
    update = z_hop(update)
    step_rows = vmem_call(pick_kernel, [place_of], [update], block_count, "pick_step_rows")
    new_params = vmem_call(step_kernel, [], [step_rows, parameters], block_count, "step")
    return step_rows, new_params


def per_device(gradients, parameters, left_root, right_root, assignment):
    plane = (assignment // (left_root.shape[0] * grid_core)) % grid_z
    loads = jnp.sum(
        (plane[None, :] == jnp.arange(grid_z, dtype=jnp.int32)[:, None]).astype(jnp.int32), axis=1
    )
    caps = jnp.array(plane_capacities[:-1], jnp.int32)
    choice = jnp.max(jnp.sum((loads[:, None] > caps[None, :]).astype(jnp.int32), axis=1))
    branches = [functools.partial(program, cap) for cap in plane_capacities]
    return lax.switch(choice, branches, gradients, parameters, left_root, right_root, assignment)


def solution(mesh):
    grid = Mesh(
        mesh.devices.reshape(grid_y, grid_z, grid_core, grid_x), ("y", "z", "core", "x")
    )
    return jax.shard_map(
        per_device,
        mesh=grid,
        in_specs=(
            P(None, fsdp_axes, "x"),
            P(None, fsdp_axes, "x"),
            P(fsdp_axes, "x", None),
            P(fsdp_axes, None, "x"),
            P(),
        ),
        out_specs=(P(None, fsdp_axes, "x"), P(None, fsdp_axes, "x")),
        check_vma=False,
    )
```

```python
import functools
import jax
import jax.numpy as jnp
from jax import lax
from jax.experimental import pallas as pl
from jax.experimental.pallas import tpu as pltpu
from jax.sharding import Mesh, PartitionSpec as P

graft_eps = 1e-06
step_rate = 0.1

grid_y, grid_z, grid_core, grid_x = 4, 16, 2, 4
plane_axes = ("y", "core", "x")
fsdp_axes = ("y", "z", "core")
plane_devices = grid_y * grid_core * grid_x
plane_capacities = (13, 15, 16, 18, 24)

pick_run = 8


def pick_kernel(index_ref, src_ref, out_ref):
    def some(step, carry):
        first = step * pick_run
        rows = [src_ref[index_ref[first + i]] for i in range(pick_run)]
        for i in range(pick_run):
            out_ref[first + i] = rows[i]
        return carry

    lax.fori_loop(0, out_ref.shape[0] // pick_run, some, 0)


def pick_runs_kernel(strides, index_ref, src_ref, out_ref):
    src_run, src_step, out_run, out_step = strides

    def one(at, carry):
        src_at, out_at = index_ref[at] * src_run, at * out_run
        for z in range(grid_z):
            out_ref[out_at + z * out_step] = src_ref[src_at + z * src_step]
        return carry

    lax.fori_loop(0, index_ref.shape[0], one, 0)


def step_kernel(step_ref, parameter_ref, new_ref):
    def some(at, carry):
        rows = pl.ds(at * pick_run, pick_run)
        new_ref[rows] = (
            parameter_ref[rows].astype(jnp.float32)
            - step_rate * step_ref[rows].astype(jnp.float32)
        ).astype(new_ref.dtype)
        return carry

    lax.fori_loop(0, new_ref.shape[0] // pick_run, some, 0)


def vmem_call(kernel, index, arrays, count, name):
    vmem_spec = pl.BlockSpec(memory_space=pltpu.VMEM)
    index_specs = [pl.BlockSpec(memory_space=pltpu.SMEM)] * len(index)
    return pl.pallas_call(
        kernel,
        out_shape=jax.ShapeDtypeStruct((count,) + arrays[0].shape[1:], arrays[0].dtype),
        in_specs=index_specs + [vmem_spec] * len(arrays),
        out_specs=vmem_spec,
        compiler_params=pltpu.CompilerParams(vmem_limit_bytes=32 * 1024 * 1024),
        name=name,
    )(*index, *arrays)


def place(values, keys, size):
    hit = jnp.arange(size, dtype=jnp.int32)[:, None] == keys[None, :]
    return jnp.sum(jnp.where(hit, values[None, :], 0), axis=1)


def holder_x(slot, core):
    return (slot + 2 + core) % grid_x


def slot_at(x, core):
    return (x + 2 * grid_x - 2 - core) % grid_x


def pack_kernel(slot_ref, left_ref, right_ref, *refs):
    sems, share = refs[-1], left_ref.shape[1]
    copies = []
    for at, out in enumerate(refs[:-1]):
        slot = slot_ref[at]
        copies.append(
            pltpu.make_async_copy(left_ref.at[slot], out.at[:share], sems.at[at * (grid_x + 1)])
        )
        for part in range(grid_x):
            span = pl.ds(part * share, share)
            copies.append(
                pltpu.make_async_copy(
                    right_ref.at[slot, span],
                    out.at[share:, span],
                    sems.at[at * (grid_x + 1) + 1 + part],
                )
            )
    for copy in copies:
        copy.start()
    for copy in copies:
        copy.wait()


def factor_pieces(left_root, right_root, here, core):
    slots, share, order = left_root.shape
    shifts = range(1, grid_x)
    wanted = jnp.stack([jnp.minimum(slot_at(here + shift, core), slots - 1) for shift in shifts])
    hbm_spec = pl.BlockSpec(memory_space=pltpu.HBM)
    packed = pl.pallas_call(
        pack_kernel,
        out_shape=[jax.ShapeDtypeStruct((2 * share, order), left_root.dtype) for shift in shifts],
        in_specs=[pl.BlockSpec(memory_space=pltpu.SMEM), hbm_spec, hbm_spec],
        out_specs=[pl.BlockSpec(memory_space=pltpu.VMEM)] * len(shifts),
        scratch_shapes=[pltpu.SemaphoreType.DMA((len(shifts) * (grid_x + 1),))],
        compiler_params=pltpu.CompilerParams(vmem_limit_bytes=32 * 1024 * 1024),
        name="pack_factors",
    )(wanted, left_root, right_root)
    got = []
    for shift, piece in zip(shifts, packed):
        pairs = [
            (at * grid_x + src, at * grid_x + (src + shift) % grid_x)
            for at in range(grid_core)
            for src in range(grid_x)
            if slot_at((src + shift) % grid_x, at) < slots
        ]
        got.append(lax.ppermute(piece, ("core", "x"), pairs))
    return got


last_sem = 2 + (grid_x - 1) * (grid_x + 1)


def slot_kernel(here_ref, *refs):
    arrived, own_left, own_right = refs[:3]
    pieces = refs[3 : 2 + grid_x]
    out, left, right, rows, block, mixed, product, staged, sems = refs[2 + grid_x :]
    here, slot = here_ref[0], here_ref[1]
    order = block.shape[0]
    share = order // grid_x
    row_local = rows.shape[2]
    pair = grid_core * row_local
    tiles = order // pair
    left_copies = [pltpu.make_async_copy(own_left.at[slot], left.at[here], sems.at[0])]
    right_copies = [pltpu.make_async_copy(own_right.at[slot], right.at[here], sems.at[1])]
    for piece in pieces:
        shift = len(left_copies)
        at = lax.rem(here - shift + grid_x, grid_x)
        first = 2 + (shift - 1) * (grid_x + 1)
        left_copies.append(
            pltpu.make_async_copy(piece.at[:share], left.at[at], sems.at[first])
        )
        for part in range(grid_x):
            span = pl.ds(part * share, share)
            right_copies.append(
                pltpu.make_async_copy(
                    piece.at[share:, span], right.at[at, span], sems.at[first + 1 + part]
                )
            )
    spans = [pl.ds(y * grid_core * grid_x, grid_core * grid_x) for y in range(grid_y)]
    row_copies = [
        pltpu.make_async_copy(arrived.at[span], rows.at[span], sems.at[last_sem + grid_y + y])
        for y, span in enumerate(spans)
    ]
    for copy in row_copies + left_copies + right_copies:
        copy.start()

    def gather_tile(tile, total):
        y, z = tile // grid_z, tile % grid_z
        at = pl.ds(pl.multiple_of(tile * pair, pair), pair)
        for x in range(grid_x):
            both = jnp.concatenate(
                [
                    rows[(y * grid_core + core) * grid_x + x, z].astype(jnp.float32)
                    for core in range(grid_core)
                ],
                axis=0,
            )
            total = total + both * both
            block[at, x * share : (x + 1) * share] = both.astype(block.dtype)
        return total

    grad_sum = jnp.zeros((pair, share), jnp.float32)
    for y in range(grid_y):
        row_copies[y].wait()
        grad_sum = lax.fori_loop(y * grid_z, (y + 1) * grid_z, gather_tile, grad_sum)
    for copy in left_copies:
        copy.wait()

    def mix(tile, carry):
        at = pl.ds(pl.multiple_of(tile * share, share), share)
        for x in range(grid_x):
            mixed[x * share : (x + 1) * share, at] = jnp.dot(
                left[x], block[:, at], preferred_element_type=jnp.float32
            ).astype(mixed.dtype)
        return carry

    lax.fori_loop(0, grid_x, mix, 0)
    for copy in right_copies:
        copy.wait()

    def finish(x, total):
        for tile in range(grid_x):
            at = slice(tile * share, (tile + 1) * share)
            part = jnp.dot(mixed[at, :], right[x], preferred_element_type=jnp.float32)
            product[x, at] = part
            total = total + jnp.sum(jnp.square(part), axis=0, keepdims=True)
        return total

    update_sum = lax.fori_loop(0, grid_x, finish, jnp.zeros((1, share), jnp.float32))
    entries = float(order * order)
    grad_ms = jnp.sum(grad_sum, axis=(0, 1), keepdims=True) / entries
    update_ms = jnp.sum(update_sum, axis=(0, 1), keepdims=True) / entries
    factor = jnp.sqrt(grad_ms + graft_eps) / jnp.sqrt(update_ms + graft_eps)

    def scatter_tile(tile, carry):
        y, z = tile // grid_z, tile % grid_z
        at = pl.ds(pl.multiple_of(tile * pair, pair), pair)
        for x in range(grid_x):
            scaled = (product[x, at, :] * factor).reshape(grid_core, row_local, share)
            for core in range(grid_core):
                staged[(y * grid_core + core) * grid_x + x, z] = scaled[core].astype(out.dtype)
        return carry

    out_copies = []
    for y, span in enumerate(spans):
        lax.fori_loop(y * grid_z, (y + 1) * grid_z, scatter_tile, 0)
        out_copies.append(
            pltpu.make_async_copy(staged.at[span], out.at[span], sems.at[last_sem + y])
        )
        out_copies[-1].start()
    for copy in out_copies:
        copy.wait()


def precondition_slot(here, core, rows, left_root, right_root, pieces):
    slots, order = right_root.shape[:2]
    share = order // grid_x
    hbm_spec = pl.BlockSpec(memory_space=pltpu.HBM)
    return pl.pallas_call(
        slot_kernel,
        out_shape=jax.ShapeDtypeStruct(rows.shape, rows.dtype),
        in_specs=[pl.BlockSpec(memory_space=pltpu.SMEM)] + [hbm_spec] * (3 + len(pieces)),
        out_specs=hbm_spec,
        scratch_shapes=[
            pltpu.VMEM((grid_x, share, order), jnp.bfloat16),
            pltpu.VMEM((grid_x, order, share), jnp.bfloat16),
            pltpu.VMEM(rows.shape, rows.dtype),
            pltpu.VMEM((order, order), jnp.bfloat16),
            pltpu.VMEM((order, order), jnp.bfloat16),
            pltpu.VMEM((grid_x, order, share), jnp.float32),
            pltpu.VMEM(rows.shape, rows.dtype),
            pltpu.SemaphoreType.DMA((last_sem + 2 * grid_y,)),
        ],
        compiler_params=pltpu.CompilerParams(vmem_limit_bytes=60 * 1024 * 1024),
        cost_estimate=pl.CostEstimate(
            flops=4 * order**3, bytes_accessed=8 * order * order, transcendentals=0
        ),
        name="precondition_slot",
    )(
        jnp.stack([here, jnp.minimum(slot_at(here, core), slots - 1)]),
        rows,
        left_root,
        right_root,
        *pieces,
    )


def program(plane_cap, gradients, parameters, left_root, right_root, assignment):
    block_count, row_local, col_local = gradients.shape
    slots_each = left_root.shape[0]
    chunk = (row_local, col_local)
    here, core = lax.axis_index("x"), lax.axis_index("core")
    pieces = factor_pieces(left_root, right_root, here, core)

    owner = assignment // slots_each
    plane = (owner // grid_core) % grid_z
    owner_core = owner % grid_core
    in_plane = ((owner // (grid_z * grid_core)) * grid_core + owner_core) * grid_x + holder_x(
        assignment % slots_each, owner_core
    )
    ids = jnp.arange(block_count, dtype=jnp.int32)
    earlier = (plane[:, None] == plane[None, :]) & (ids[None, :] < ids[:, None])
    rank = jnp.sum(earlier.astype(jnp.int32), axis=1)
    place_of = plane * plane_cap + rank
    my_z = lax.axis_index("z")
    block_at = place(ids, place_of, grid_z * plane_cap)
    mine = plane == my_z
    rank_at = place(rank, jnp.where(mine, in_plane, plane_devices), plane_devices)
    holder_at = place(in_plane, jnp.where(mine, rank, plane_cap), plane_cap)
    plane_rows, z_rows = plane_devices * grid_z, grid_z * plane_cap

    def z_hop(rows):
        rows = rows.reshape((grid_z, plane_cap) + chunk)
        return lax.all_to_all(rows, "z", 0, 0, tiled=True).reshape((z_rows,) + chunk)

    def plane_hop(rows):
        rows = rows.reshape((plane_devices, grid_z) + chunk)
        return lax.all_to_all(rows, plane_axes, 0, 0, tiled=True)

    rows = vmem_call(pick_kernel, [block_at], [gradients], z_rows, "pick_for_z")
    rows, pieces = lax.optimization_barrier((z_hop(rows), pieces))
    kernel = functools.partial(pick_runs_kernel, (1, plane_cap, grid_z, 1))
    rows = vmem_call(kernel, [rank_at], [rows], plane_rows, "pick_for_plane")
    rows = plane_hop(rows)
    update = precondition_slot(here, core, rows, left_root, right_root, pieces)
    update = plane_hop(update).reshape((plane_rows,) + chunk)
    kernel = functools.partial(pick_runs_kernel, (grid_z, 1, 1, plane_cap))
    update = vmem_call(kernel, [holder_at], [update], z_rows, "pick_back_for_z")
    update = z_hop(update)
    step_rows = vmem_call(pick_kernel, [place_of], [update], block_count, "pick_step_rows")
    new_params = vmem_call(step_kernel, [], [step_rows, parameters], block_count, "step")
    return step_rows, new_params


def per_device(gradients, parameters, left_root, right_root, assignment):
    plane = (assignment // (left_root.shape[0] * grid_core)) % grid_z
    loads = jnp.sum(
        (plane[None, :] == jnp.arange(grid_z, dtype=jnp.int32)[:, None]).astype(jnp.int32), axis=1
    )
    caps = jnp.array(plane_capacities[:-1], jnp.int32)
    choice = jnp.max(jnp.sum((loads[:, None] > caps[None, :]).astype(jnp.int32), axis=1))
    branches = [functools.partial(program, cap) for cap in plane_capacities]
    return lax.switch(choice, branches, gradients, parameters, left_root, right_root, assignment)


def solution(mesh):
    grid = Mesh(
        mesh.devices.reshape(grid_y, grid_z, grid_core, grid_x), ("y", "z", "core", "x")
    )
    return jax.shard_map(
        per_device,
        mesh=grid,
        in_specs=(
            P(None, fsdp_axes, "x"),
            P(None, fsdp_axes, "x"),
            P(fsdp_axes, "x", None),
            P(fsdp_axes, None, "x"),
            P(),
        ),
        out_specs=(P(None, fsdp_axes, "x"), P(None, fsdp_axes, "x")),
        check_vma=False,
    )
```

```python
import functools
import jax
import jax.numpy as jnp
from jax import lax
from jax.experimental import pallas as pl
from jax.experimental.pallas import tpu as pltpu
from jax.sharding import Mesh, PartitionSpec as P

graft_eps = 1e-06
step_rate = 0.1

grid_y, grid_z, grid_core, grid_x = 4, 16, 2, 4
plane_axes = ("y", "core", "x")
fsdp_axes = ("y", "z", "core")
plane_devices = grid_y * grid_core * grid_x
plane_capacities = (13, 14, 15, 16, 18, 24)

pick_run = 8


def pick_kernel(index_ref, src_ref, out_ref):
    def some(step, carry):
        first = step * pick_run
        rows = [src_ref[index_ref[first + i]] for i in range(pick_run)]
        for i in range(pick_run):
            out_ref[first + i] = rows[i]
        return carry

    lax.fori_loop(0, out_ref.shape[0] // pick_run, some, 0)


def pick_runs_kernel(strides, index_ref, src_ref, out_ref):
    src_run, src_step, out_run, out_step = strides

    def one(at, carry):
        src_at, out_at = index_ref[at] * src_run, at * out_run
        for z in range(grid_z):
            out_ref[out_at + z * out_step] = src_ref[src_at + z * src_step]
        return carry

    lax.fori_loop(0, index_ref.shape[0], one, 0)


def step_kernel(step_ref, parameter_ref, new_ref):
    def some(at, carry):
        rows = pl.ds(at * pick_run, pick_run)
        new_ref[rows] = (
            parameter_ref[rows].astype(jnp.float32)
            - step_rate * step_ref[rows].astype(jnp.float32)
        ).astype(new_ref.dtype)
        return carry

    lax.fori_loop(0, new_ref.shape[0] // pick_run, some, 0)


def vmem_call(kernel, index, arrays, count, name):
    vmem_spec = pl.BlockSpec(memory_space=pltpu.VMEM)
    index_specs = [pl.BlockSpec(memory_space=pltpu.SMEM)] * len(index)
    return pl.pallas_call(
        kernel,
        out_shape=jax.ShapeDtypeStruct((count,) + arrays[0].shape[1:], arrays[0].dtype),
        in_specs=index_specs + [vmem_spec] * len(arrays),
        out_specs=vmem_spec,
        compiler_params=pltpu.CompilerParams(vmem_limit_bytes=32 * 1024 * 1024),
        name=name,
    )(*index, *arrays)


def place(values, keys, size):
    hit = jnp.arange(size, dtype=jnp.int32)[:, None] == keys[None, :]
    return jnp.sum(jnp.where(hit, values[None, :], 0), axis=1)


piece_shifts = (2, 3, 1)


def holder_x(slot, core):
    return (slot + 2 + core) % grid_x


def slot_at(x, core):
    return (x + 2 * grid_x - 2 - core) % grid_x


def pack_kernel(slot_ref, left_ref, right_ref, *refs):
    sems, share = refs[-1], left_ref.shape[1]
    copies = []
    for at, out in enumerate(refs[:-1]):
        slot = slot_ref[at]
        copies.append(
            pltpu.make_async_copy(left_ref.at[slot], out.at[:share], sems.at[at * (grid_x + 1)])
        )
        for part in range(grid_x):
            span = pl.ds(part * share, share)
            copies.append(
                pltpu.make_async_copy(
                    right_ref.at[slot, span],
                    out.at[share:, span],
                    sems.at[at * (grid_x + 1) + 1 + part],
                )
            )
    for copy in copies:
        copy.start()
    for copy in copies:
        copy.wait()


def factor_pieces(left_root, right_root, here, core):
    slots, share, order = left_root.shape
    wanted = jnp.stack(
        [jnp.minimum(slot_at(here + shift, core), slots - 1) for shift in piece_shifts]
    )
    hbm_spec = pl.BlockSpec(memory_space=pltpu.HBM)
    packed = pl.pallas_call(
        pack_kernel,
        out_shape=[jax.ShapeDtypeStruct((2 * share, order), left_root.dtype)] * len(piece_shifts),
        in_specs=[pl.BlockSpec(memory_space=pltpu.SMEM), hbm_spec, hbm_spec],
        out_specs=[pl.BlockSpec(memory_space=pltpu.VMEM)] * len(piece_shifts),
        scratch_shapes=[pltpu.SemaphoreType.DMA((len(piece_shifts) * (grid_x + 1),))],
        compiler_params=pltpu.CompilerParams(vmem_limit_bytes=32 * 1024 * 1024),
        name="pack_factors",
    )(wanted, left_root, right_root)
    got = []
    for shift, piece in zip(piece_shifts, packed):
        pairs = [
            (at * grid_x + src, at * grid_x + (src + shift) % grid_x)
            for at in range(grid_core)
            for src in range(grid_x)
            if slot_at((src + shift) % grid_x, at) < slots
        ]
        got.append(lax.ppermute(piece, ("core", "x"), pairs))
    return got


last_sem = 2 + (grid_x - 1) * (grid_x + 1)


def slot_kernel(here_ref, *refs):
    arrived, own_left, own_right = refs[:3]
    pieces = refs[3 : 2 + grid_x]
    out, left, right, rows, block, mixed, product, staged, sems = refs[2 + grid_x :]
    here, slot = here_ref[0], here_ref[1]
    order = block.shape[0]
    share = order // grid_x
    row_local = rows.shape[2]
    pair = grid_core * row_local
    tiles = order // pair
    left_copies = [pltpu.make_async_copy(own_left.at[slot], left.at[here], sems.at[0])]
    right_copies = [pltpu.make_async_copy(own_right.at[slot], right.at[here], sems.at[1])]
    for number, piece in enumerate(pieces):
        at = lax.rem(here - piece_shifts[number] + grid_x, grid_x)
        first = 2 + number * (grid_x + 1)
        left_copies.append(
            pltpu.make_async_copy(piece.at[:share], left.at[at], sems.at[first])
        )
        for part in range(grid_x):
            span = pl.ds(part * share, share)
            right_copies.append(
                pltpu.make_async_copy(
                    piece.at[share:, span], right.at[at, span], sems.at[first + 1 + part]
                )
            )
    spans = [pl.ds(y * grid_core * grid_x, grid_core * grid_x) for y in range(grid_y)]
    row_copies = [
        pltpu.make_async_copy(arrived.at[span], rows.at[span], sems.at[last_sem + grid_y + y])
        for y, span in enumerate(spans)
    ]
    for copy in row_copies + left_copies + right_copies:
        copy.start()

    def gather_tile(tile, total):
        y, z = tile // grid_z, tile % grid_z
        at = pl.ds(pl.multiple_of(tile * pair, pair), pair)
        for x in range(grid_x):
            both = jnp.concatenate(
                [
                    rows[(y * grid_core + core) * grid_x + x, z].astype(jnp.float32)
                    for core in range(grid_core)
                ],
                axis=0,
            )
            total = total + both * both
            block[at, x * share : (x + 1) * share] = both.astype(block.dtype)
        return total

    grad_sum = jnp.zeros((pair, share), jnp.float32)
    for y in range(grid_y):
        row_copies[y].wait()
        grad_sum = lax.fori_loop(y * grid_z, (y + 1) * grid_z, gather_tile, grad_sum)
    for copy in left_copies:
        copy.wait()

    def mix(tile, carry):
        at = pl.ds(pl.multiple_of(tile * share, share), share)
        mixed[:, at] = jnp.dot(
            left[...].reshape(order, order), block[:, at], preferred_element_type=jnp.float32
        ).astype(mixed.dtype)
        return carry

    lax.fori_loop(0, grid_x, mix, 0)
    for copy in right_copies:
        copy.wait()

    def finish(x, total):
        part = jnp.dot(mixed[...], right[x], preferred_element_type=jnp.float32)
        product[x] = part
        return total + jnp.sum(jnp.square(part), axis=0, keepdims=True)

    update_sum = lax.fori_loop(0, grid_x, finish, jnp.zeros((1, share), jnp.float32))
    entries = float(order * order)
    grad_ms = jnp.sum(grad_sum, axis=(0, 1), keepdims=True) / entries
    update_ms = jnp.sum(update_sum, axis=(0, 1), keepdims=True) / entries
    factor = jnp.sqrt(grad_ms + graft_eps) / jnp.sqrt(update_ms + graft_eps)

    def scatter_tile(tile, carry):
        y, z = tile // grid_z, tile % grid_z
        at = pl.ds(pl.multiple_of(tile * pair, pair), pair)
        for x in range(grid_x):
            scaled = (product[x, at, :] * factor).reshape(grid_core, row_local, share)
            for core in range(grid_core):
                staged[(y * grid_core + core) * grid_x + x, z] = scaled[core].astype(out.dtype)
        return carry

    out_copies = []
    for y, span in enumerate(spans):
        lax.fori_loop(y * grid_z, (y + 1) * grid_z, scatter_tile, 0)
        out_copies.append(
            pltpu.make_async_copy(staged.at[span], out.at[span], sems.at[last_sem + y])
        )
        out_copies[-1].start()
    for copy in out_copies:
        copy.wait()


def precondition_slot(here, core, rows, left_root, right_root, pieces):
    slots, order = right_root.shape[:2]
    share = order // grid_x
    hbm_spec = pl.BlockSpec(memory_space=pltpu.HBM)
    return pl.pallas_call(
        slot_kernel,
        out_shape=jax.ShapeDtypeStruct(rows.shape, rows.dtype),
        in_specs=[pl.BlockSpec(memory_space=pltpu.SMEM)] + [hbm_spec] * (3 + len(pieces)),
        out_specs=hbm_spec,
        scratch_shapes=[
            pltpu.VMEM((grid_x, share, order), jnp.bfloat16),
            pltpu.VMEM((grid_x, order, share), jnp.bfloat16),
            pltpu.VMEM(rows.shape, rows.dtype),
            pltpu.VMEM((order, order), jnp.bfloat16),
            pltpu.VMEM((order, order), jnp.bfloat16),
            pltpu.VMEM((grid_x, order, share), jnp.float32),
            pltpu.VMEM(rows.shape, rows.dtype),
            pltpu.SemaphoreType.DMA((last_sem + 2 * grid_y,)),
        ],
        compiler_params=pltpu.CompilerParams(vmem_limit_bytes=60 * 1024 * 1024),
        cost_estimate=pl.CostEstimate(
            flops=4 * order**3, bytes_accessed=8 * order * order, transcendentals=0
        ),
        name="precondition_slot",
    )(
        jnp.stack([here, jnp.minimum(slot_at(here, core), slots - 1)]),
        rows,
        left_root,
        right_root,
        *pieces,
    )


def program(plane_cap, gradients, parameters, left_root, right_root, assignment):
    block_count, row_local, col_local = gradients.shape
    slots_each = left_root.shape[0]
    chunk = (row_local, col_local)
    here, core = lax.axis_index("x"), lax.axis_index("core")
    pieces = factor_pieces(left_root, right_root, here, core)

    owner = assignment // slots_each
    plane = (owner // grid_core) % grid_z
    owner_core = owner % grid_core
    in_plane = ((owner // (grid_z * grid_core)) * grid_core + owner_core) * grid_x + holder_x(
        assignment % slots_each, owner_core
    )
    ids = jnp.arange(block_count, dtype=jnp.int32)
    earlier = (plane[:, None] == plane[None, :]) & (ids[None, :] < ids[:, None])
    rank = jnp.sum(earlier.astype(jnp.int32), axis=1)
    place_of = plane * plane_cap + rank
    my_z = lax.axis_index("z")
    block_at = place(ids, place_of, grid_z * plane_cap)
    mine = plane == my_z
    rank_at = place(rank, jnp.where(mine, in_plane, plane_devices), plane_devices)
    holder_at = place(in_plane, jnp.where(mine, rank, plane_cap), plane_cap)
    plane_rows, z_rows = plane_devices * grid_z, grid_z * plane_cap

    def z_hop(rows):
        rows = rows.reshape((grid_z, plane_cap) + chunk)
        return lax.all_to_all(rows, "z", 0, 0, tiled=True).reshape((z_rows,) + chunk)

    def plane_hop(rows):
        rows = rows.reshape((plane_devices, grid_z) + chunk)
        return lax.all_to_all(rows, plane_axes, 0, 0, tiled=True)

    rows = vmem_call(pick_kernel, [block_at], [gradients], z_rows, "pick_for_z")
    rows, pieces = lax.optimization_barrier((z_hop(rows), pieces))
    kernel = functools.partial(pick_runs_kernel, (1, plane_cap, grid_z, 1))
    rows = vmem_call(kernel, [rank_at], [rows], plane_rows, "pick_for_plane")
    rows = plane_hop(rows)
    update = precondition_slot(here, core, rows, left_root, right_root, pieces)
    update = plane_hop(update).reshape((plane_rows,) + chunk)
    kernel = functools.partial(pick_runs_kernel, (grid_z, 1, 1, plane_cap))
    update = vmem_call(kernel, [holder_at], [update], z_rows, "pick_back_for_z")
    update = z_hop(update)
    step_rows = vmem_call(pick_kernel, [place_of], [update], block_count, "pick_step_rows")
    new_params = vmem_call(step_kernel, [], [step_rows, parameters], block_count, "step")
    return step_rows, new_params


def per_device(gradients, parameters, left_root, right_root, assignment):
    plane = (assignment // (left_root.shape[0] * grid_core)) % grid_z
    loads = jnp.sum(
        (plane[None, :] == jnp.arange(grid_z, dtype=jnp.int32)[:, None]).astype(jnp.int32), axis=1
    )
    choice = jnp.max(sum((loads > cap).astype(jnp.int32) for cap in plane_capacities[:-1]))
    branches = [functools.partial(program, cap) for cap in plane_capacities]
    return lax.switch(choice, branches, gradients, parameters, left_root, right_root, assignment)


def solution(mesh):
    grid = Mesh(
        mesh.devices.reshape(grid_y, grid_z, grid_core, grid_x), ("y", "z", "core", "x")
    )
    return jax.shard_map(
        per_device,
        mesh=grid,
        in_specs=(
            P(None, fsdp_axes, "x"),
            P(None, fsdp_axes, "x"),
            P(fsdp_axes, "x", None),
            P(fsdp_axes, None, "x"),
            P(),
        ),
        out_specs=(P(None, fsdp_axes, "x"), P(None, fsdp_axes, "x")),
        check_vma=False,
    )
```

```python
import functools
import jax
import jax.numpy as jnp
from jax import lax
from jax.experimental import pallas as pl
from jax.experimental.pallas import tpu as pltpu
from jax.sharding import Mesh, PartitionSpec as P

graft_eps = 1e-06
step_rate = 0.1

grid_y, grid_z, grid_core, grid_x = 4, 16, 2, 4
plane_axes = ("y", "core", "x")
fsdp_axes = ("y", "z", "core")
plane_devices = grid_y * grid_core * grid_x
plane_capacities = (13, 14, 15, 16, 18, 24)

pick_run = 8


def pick_kernel(index_ref, src_ref, out_ref):
    def some(step, carry):
        first = step * pick_run
        rows = [src_ref[index_ref[first + i]] for i in range(pick_run)]
        for i in range(pick_run):
            out_ref[first + i] = rows[i]
        return carry

    lax.fori_loop(0, out_ref.shape[0] // pick_run, some, 0)


def pick_runs_kernel(strides, index_ref, src_ref, out_ref):
    src_run, src_step, out_run, out_step = strides

    def one(at, carry):
        src_at, out_at = index_ref[at] * src_run, at * out_run
        for z in range(grid_z):
            out_ref[out_at + z * out_step] = src_ref[src_at + z * src_step]
        return carry

    lax.fori_loop(0, index_ref.shape[0], one, 0)


def step_kernel(step_ref, parameter_ref, new_ref):
    def some(at, carry):
        rows = pl.ds(at * pick_run, pick_run)
        new_ref[rows] = (
            parameter_ref[rows].astype(jnp.float32)
            - step_rate * step_ref[rows].astype(jnp.float32)
        ).astype(new_ref.dtype)
        return carry

    lax.fori_loop(0, new_ref.shape[0] // pick_run, some, 0)


def vmem_call(kernel, index, arrays, count, name):
    vmem_spec = pl.BlockSpec(memory_space=pltpu.VMEM)
    index_specs = [pl.BlockSpec(memory_space=pltpu.SMEM)] * len(index)
    return pl.pallas_call(
        kernel,
        out_shape=jax.ShapeDtypeStruct((count,) + arrays[0].shape[1:], arrays[0].dtype),
        in_specs=index_specs + [vmem_spec] * len(arrays),
        out_specs=vmem_spec,
        compiler_params=pltpu.CompilerParams(vmem_limit_bytes=32 * 1024 * 1024),
        name=name,
    )(*index, *arrays)


def place(values, keys, size):
    hit = jnp.arange(size, dtype=jnp.int32)[:, None] == keys[None, :]
    return jnp.sum(jnp.where(hit, values[None, :], 0), axis=1)


piece_shifts = (2, 3, 1)


def holder_x(slot, core):
    return (slot + 2 + core) % grid_x


def slot_at(x, core):
    return (x + 2 * grid_x - 2 - core) % grid_x


def pack_kernel(slot_ref, left_ref, right_ref, *refs):
    sems, share = refs[-1], left_ref.shape[1]
    copies = []
    for at, out in enumerate(refs[:-1]):
        slot = slot_ref[at]
        copies.append(
            pltpu.make_async_copy(left_ref.at[slot], out.at[:share], sems.at[at * (grid_x + 1)])
        )
        for part in range(grid_x):
            span = pl.ds(part * share, share)
            copies.append(
                pltpu.make_async_copy(
                    right_ref.at[slot, span],
                    out.at[share:, span],
                    sems.at[at * (grid_x + 1) + 1 + part],
                )
            )
    for copy in copies:
        copy.start()
    for copy in copies:
        copy.wait()


def factor_pieces(left_root, right_root, here, core):
    slots, share, order = left_root.shape
    wanted = jnp.stack(
        [jnp.minimum(slot_at(here + shift, core), slots - 1) for shift in piece_shifts]
    )
    hbm_spec = pl.BlockSpec(memory_space=pltpu.HBM)
    packed = pl.pallas_call(
        pack_kernel,
        out_shape=[jax.ShapeDtypeStruct((2 * share, order), left_root.dtype)] * len(piece_shifts),
        in_specs=[pl.BlockSpec(memory_space=pltpu.SMEM), hbm_spec, hbm_spec],
        out_specs=[pl.BlockSpec(memory_space=pltpu.VMEM)] * len(piece_shifts),
        scratch_shapes=[pltpu.SemaphoreType.DMA((len(piece_shifts) * (grid_x + 1),))],
        compiler_params=pltpu.CompilerParams(vmem_limit_bytes=32 * 1024 * 1024),
        name="pack_factors",
    )(wanted, left_root, right_root)
    got = []
    for shift, piece in zip(piece_shifts, packed):
        pairs = [
            (at * grid_x + src, at * grid_x + (src + shift) % grid_x)
            for at in range(grid_core)
            for src in range(grid_x)
            if slot_at((src + shift) % grid_x, at) < slots
        ]
        got.append(lax.ppermute(piece, ("core", "x"), pairs))
    return got


last_sem = 2 + (grid_x - 1) * (grid_x + 1)


def slot_kernel(here_ref, *refs):
    arrived, own_left, own_right = refs[:3]
    pieces = refs[3 : 2 + grid_x]
    out, left, right, rows, block, mixed, product, staged, sems = refs[2 + grid_x :]
    here, slot = here_ref[0], here_ref[1]
    order = block.shape[0]
    share = order // grid_x
    row_local = rows.shape[2]
    pair = grid_core * row_local
    tiles = order // pair
    left_copies = [pltpu.make_async_copy(own_left.at[slot], left.at[here], sems.at[0])]
    right_copies = [pltpu.make_async_copy(own_right.at[slot], right.at[here], sems.at[1])]
    for number, piece in enumerate(pieces):
        at = lax.rem(here - piece_shifts[number] + grid_x, grid_x)
        first = 2 + number * (grid_x + 1)
        left_copies.append(
            pltpu.make_async_copy(piece.at[:share], left.at[at], sems.at[first])
        )
        for part in range(grid_x):
            span = pl.ds(part * share, share)
            right_copies.append(
                pltpu.make_async_copy(
                    piece.at[share:, span], right.at[at, span], sems.at[first + 1 + part]
                )
            )
    spans = [pl.ds(y * grid_core * grid_x, grid_core * grid_x) for y in range(grid_y)]
    row_copies = [
        pltpu.make_async_copy(arrived.at[span], rows.at[span], sems.at[last_sem + grid_y + y])
        for y, span in enumerate(spans)
    ]
    for copy in row_copies + left_copies + right_copies:
        copy.start()

    def gather_tile(tile, total):
        y, z = tile // grid_z, tile % grid_z
        at = pl.ds(pl.multiple_of(tile * pair, pair), pair)
        for x in range(grid_x):
            both = jnp.concatenate(
                [
                    rows[(y * grid_core + core) * grid_x + x, z].astype(jnp.float32)
                    for core in range(grid_core)
                ],
                axis=0,
            )
            total = total + both * both
            block[at, x * share : (x + 1) * share] = both.astype(block.dtype)
        return total

    grad_sum = jnp.zeros((pair, share), jnp.float32)
    for y in range(grid_y):
        row_copies[y].wait()
        grad_sum = lax.fori_loop(
            y * grid_z, (y + 1) * grid_z, gather_tile, grad_sum, unroll=4
        )
    for copy in left_copies:
        copy.wait()

    def mix(tile, carry):
        at = pl.ds(pl.multiple_of(tile * share, share), share)
        mixed[:, at] = jnp.dot(
            left[...].reshape(order, order), block[:, at], preferred_element_type=jnp.float32
        ).astype(mixed.dtype)
        return carry

    lax.fori_loop(0, grid_x, mix, 0)
    for copy in right_copies:
        copy.wait()

    def finish(x, total):
        part = jnp.dot(mixed[...], right[x], preferred_element_type=jnp.float32)
        product[x] = part
        return total + jnp.sum(jnp.square(part), axis=0, keepdims=True)

    update_sum = lax.fori_loop(0, grid_x, finish, jnp.zeros((1, share), jnp.float32))
    entries = float(order * order)
    grad_ms = jnp.sum(grad_sum, axis=(0, 1), keepdims=True) / entries
    update_ms = jnp.sum(update_sum, axis=(0, 1), keepdims=True) / entries
    factor = jnp.sqrt(grad_ms + graft_eps) / jnp.sqrt(update_ms + graft_eps)

    def scatter_tile(tile, carry):
        y, z = tile // grid_z, tile % grid_z
        at = pl.ds(pl.multiple_of(tile * pair, pair), pair)
        for x in range(grid_x):
            scaled = (product[x, at, :] * factor).reshape(grid_core, row_local, share)
            for core in range(grid_core):
                staged[(y * grid_core + core) * grid_x + x, z] = scaled[core].astype(out.dtype)
        return carry

    out_copies = []
    for y, span in enumerate(spans):
        lax.fori_loop(y * grid_z, (y + 1) * grid_z, scatter_tile, 0, unroll=4)
        out_copies.append(
            pltpu.make_async_copy(staged.at[span], out.at[span], sems.at[last_sem + y])
        )
        out_copies[-1].start()
    for copy in out_copies:
        copy.wait()


def precondition_slot(here, core, rows, left_root, right_root, pieces):
    slots, order = right_root.shape[:2]
    share = order // grid_x
    hbm_spec = pl.BlockSpec(memory_space=pltpu.HBM)
    return pl.pallas_call(
        slot_kernel,
        out_shape=jax.ShapeDtypeStruct(rows.shape, rows.dtype),
        in_specs=[pl.BlockSpec(memory_space=pltpu.SMEM)] + [hbm_spec] * (3 + len(pieces)),
        out_specs=hbm_spec,
        scratch_shapes=[
            pltpu.VMEM((grid_x, share, order), jnp.bfloat16),
            pltpu.VMEM((grid_x, order, share), jnp.bfloat16),
            pltpu.VMEM(rows.shape, rows.dtype),
            pltpu.VMEM((order, order), jnp.bfloat16),
            pltpu.VMEM((order, order), jnp.bfloat16),
            pltpu.VMEM((grid_x, order, share), jnp.float32),
            pltpu.VMEM(rows.shape, rows.dtype),
            pltpu.SemaphoreType.DMA((last_sem + 2 * grid_y,)),
        ],
        compiler_params=pltpu.CompilerParams(vmem_limit_bytes=60 * 1024 * 1024),
        cost_estimate=pl.CostEstimate(
            flops=4 * order**3, bytes_accessed=8 * order * order, transcendentals=0
        ),
        name="precondition_slot",
    )(
        jnp.stack([here, jnp.minimum(slot_at(here, core), slots - 1)]),
        rows,
        left_root,
        right_root,
        *pieces,
    )


def program(plane_cap, gradients, parameters, left_root, right_root, assignment):
    block_count, row_local, col_local = gradients.shape
    slots_each = left_root.shape[0]
    chunk = (row_local, col_local)
    here, core = lax.axis_index("x"), lax.axis_index("core")
    pieces = factor_pieces(left_root, right_root, here, core)

    owner = assignment // slots_each
    plane = (owner // grid_core) % grid_z
    owner_core = owner % grid_core
    in_plane = ((owner // (grid_z * grid_core)) * grid_core + owner_core) * grid_x + holder_x(
        assignment % slots_each, owner_core
    )
    ids = jnp.arange(block_count, dtype=jnp.int32)
    earlier = (plane[:, None] == plane[None, :]) & (ids[None, :] < ids[:, None])
    rank = jnp.sum(earlier.astype(jnp.int32), axis=1)
    place_of = plane * plane_cap + rank
    my_z = lax.axis_index("z")
    block_at = place(ids, place_of, grid_z * plane_cap)
    mine = plane == my_z
    rank_at = place(rank, jnp.where(mine, in_plane, plane_devices), plane_devices)
    holder_at = place(in_plane, jnp.where(mine, rank, plane_cap), plane_cap)
    plane_rows, z_rows = plane_devices * grid_z, grid_z * plane_cap

    def z_hop(rows):
        rows = rows.reshape((grid_z, plane_cap) + chunk)
        return lax.all_to_all(rows, "z", 0, 0, tiled=True).reshape((z_rows,) + chunk)

    def plane_hop(rows):
        rows = rows.reshape((plane_devices, grid_z) + chunk)
        return lax.all_to_all(rows, plane_axes, 0, 0, tiled=True)

    rows = vmem_call(pick_kernel, [block_at], [gradients], z_rows, "pick_for_z")
    kernel = functools.partial(pick_runs_kernel, (1, plane_cap, grid_z, 1))
    rows = vmem_call(kernel, [rank_at], [z_hop(rows)], plane_rows, "pick_for_plane")
    rows, pieces = lax.optimization_barrier((rows, pieces))
    rows = plane_hop(rows)
    update = precondition_slot(here, core, rows, left_root, right_root, pieces)
    update = plane_hop(update).reshape((plane_rows,) + chunk)
    kernel = functools.partial(pick_runs_kernel, (grid_z, 1, 1, plane_cap))
    update = vmem_call(kernel, [holder_at], [update], z_rows, "pick_back_for_z")
    update = z_hop(update)
    step_rows = vmem_call(pick_kernel, [place_of], [update], block_count, "pick_step_rows")
    new_params = vmem_call(step_kernel, [], [step_rows, parameters], block_count, "step")
    return step_rows, new_params


def per_device(gradients, parameters, left_root, right_root, assignment):
    plane = (assignment // (left_root.shape[0] * grid_core)) % grid_z
    loads = jnp.sum(
        (plane[None, :] == jnp.arange(grid_z, dtype=jnp.int32)[:, None]).astype(jnp.int32), axis=1
    )
    choice = jnp.max(sum((loads > cap).astype(jnp.int32) for cap in plane_capacities[:-1]))
    branches = [functools.partial(program, cap) for cap in plane_capacities]
    return lax.switch(choice, branches, gradients, parameters, left_root, right_root, assignment)


def solution(mesh):
    grid = Mesh(
        mesh.devices.reshape(grid_y, grid_z, grid_core, grid_x), ("y", "z", "core", "x")
    )
    return jax.shard_map(
        per_device,
        mesh=grid,
        in_specs=(
            P(None, fsdp_axes, "x"),
            P(None, fsdp_axes, "x"),
            P(fsdp_axes, "x", None),
            P(fsdp_axes, None, "x"),
            P(),
        ),
        out_specs=(P(None, fsdp_axes, "x"), P(None, fsdp_axes, "x")),
        check_vma=False,
    )
```

```python
import functools
import jax
import jax.numpy as jnp
from jax import lax
from jax.experimental import pallas as pl
from jax.experimental.pallas import tpu as pltpu
from jax.sharding import Mesh, PartitionSpec as P

graft_eps = 1e-06
step_rate = 0.1

grid_y, grid_z, grid_core, grid_x = 4, 16, 2, 4
plane_axes = ("y", "core", "x")
fsdp_axes = ("y", "z", "core")
plane_devices = grid_y * grid_core * grid_x
plane_capacities = (13, 14, 15, 16, 18, 24)

pick_run = 8


def pick_kernel(index_ref, src_ref, out_ref):
    def some(step, carry):
        first = step * pick_run
        rows = [src_ref[index_ref[first + i]] for i in range(pick_run)]
        for i in range(pick_run):
            out_ref[first + i] = rows[i]
        return carry

    lax.fori_loop(0, out_ref.shape[0] // pick_run, some, 0)


def pick_runs_kernel(strides, index_ref, src_ref, out_ref):
    src_run, src_step, out_run, out_step = strides

    def one(at, carry):
        src_at, out_at = index_ref[at] * src_run, at * out_run
        for z in range(grid_z):
            out_ref[out_at + z * out_step] = src_ref[src_at + z * src_step]
        return carry

    lax.fori_loop(0, index_ref.shape[0], one, 0)


def step_kernel(step_ref, parameter_ref, new_ref):
    def some(at, carry):
        rows = pl.ds(at * pick_run, pick_run)
        new_ref[rows] = (
            parameter_ref[rows].astype(jnp.float32)
            - step_rate * step_ref[rows].astype(jnp.float32)
        ).astype(new_ref.dtype)
        return carry

    lax.fori_loop(0, new_ref.shape[0] // pick_run, some, 0)


def vmem_call(kernel, index, arrays, count, name):
    vmem_spec = pl.BlockSpec(memory_space=pltpu.VMEM)
    index_specs = [pl.BlockSpec(memory_space=pltpu.SMEM)] * len(index)
    return pl.pallas_call(
        kernel,
        out_shape=jax.ShapeDtypeStruct((count,) + arrays[0].shape[1:], arrays[0].dtype),
        in_specs=index_specs + [vmem_spec] * len(arrays),
        out_specs=vmem_spec,
        compiler_params=pltpu.CompilerParams(vmem_limit_bytes=32 * 1024 * 1024),
        name=name,
    )(*index, *arrays)


def place(values, keys, size):
    hit = jnp.arange(size, dtype=jnp.int32)[:, None] == keys[None, :]
    return jnp.sum(jnp.where(hit, values[None, :], 0), axis=1)


piece_shifts = (2, 3, 1)


def holder_x(slot, core):
    return (slot + 2 + core) % grid_x


def slot_at(x, core):
    return (x + 2 * grid_x - 2 - core) % grid_x


def pack_kernel(slot_ref, left_ref, right_ref, *refs):
    sems, share = refs[-1], left_ref.shape[1]
    copies = []
    for at, out in enumerate(refs[:-1]):
        slot = slot_ref[at]
        copies.append(
            pltpu.make_async_copy(left_ref.at[slot], out.at[:share], sems.at[at * (grid_x + 1)])
        )
        for part in range(grid_x):
            span = pl.ds(part * share, share)
            copies.append(
                pltpu.make_async_copy(
                    right_ref.at[slot, span],
                    out.at[share:, span],
                    sems.at[at * (grid_x + 1) + 1 + part],
                )
            )
    for copy in copies:
        copy.start()
    for copy in copies:
        copy.wait()


def factor_pieces(left_root, right_root, here, core):
    slots, share, order = left_root.shape
    wanted = jnp.stack(
        [jnp.minimum(slot_at(here + shift, core), slots - 1) for shift in piece_shifts]
    )
    hbm_spec = pl.BlockSpec(memory_space=pltpu.HBM)
    packed = pl.pallas_call(
        pack_kernel,
        out_shape=[jax.ShapeDtypeStruct((2 * share, order), left_root.dtype)] * len(piece_shifts),
        in_specs=[pl.BlockSpec(memory_space=pltpu.SMEM), hbm_spec, hbm_spec],
        out_specs=[pl.BlockSpec(memory_space=pltpu.VMEM)] * len(piece_shifts),
        scratch_shapes=[pltpu.SemaphoreType.DMA((len(piece_shifts) * (grid_x + 1),))],
        compiler_params=pltpu.CompilerParams(vmem_limit_bytes=32 * 1024 * 1024),
        name="pack_factors",
    )(wanted, left_root, right_root)
    got = []
    for shift, piece in zip(piece_shifts, packed):
        pairs = [
            (at * grid_x + src, at * grid_x + (src + shift) % grid_x)
            for at in range(grid_core)
            for src in range(grid_x)
            if slot_at((src + shift) % grid_x, at) < slots
        ]
        got.append(lax.ppermute(piece, ("core", "x"), pairs))
    return got


last_sem = 2 + (grid_x - 1) * (grid_x + 1)


def slot_kernel(here_ref, *refs):
    arrived, own_left, own_right = refs[:3]
    pieces = refs[3 : 2 + grid_x]
    out, left, right, rows, mixed, product, staged, sems = refs[2 + grid_x : -grid_x]
    blocks = refs[-grid_x:]
    here, slot = here_ref[0], here_ref[1]
    order = mixed.shape[0]
    share = order // grid_x
    row_local = rows.shape[2]
    pair = grid_core * row_local
    tiles = order // pair
    left_copies = [pltpu.make_async_copy(own_left.at[slot], left.at[here], sems.at[0])]
    right_copies = [pltpu.make_async_copy(own_right.at[slot], right.at[here], sems.at[1])]
    for number, piece in enumerate(pieces):
        at = lax.rem(here - piece_shifts[number] + grid_x, grid_x)
        first = 2 + number * (grid_x + 1)
        left_copies.append(
            pltpu.make_async_copy(piece.at[:share], left.at[at], sems.at[first])
        )
        for part in range(grid_x):
            span = pl.ds(part * share, share)
            right_copies.append(
                pltpu.make_async_copy(
                    piece.at[share:, span], right.at[at, span], sems.at[first + 1 + part]
                )
            )
    spans = [pl.ds(y * grid_core * grid_x, grid_core * grid_x) for y in range(grid_y)]
    row_copies = [
        pltpu.make_async_copy(arrived.at[span], rows.at[span], sems.at[last_sem + grid_y + y])
        for y, span in enumerate(spans)
    ]
    for copy in row_copies + left_copies + right_copies:
        copy.start()

    def gather(x, y, total):
        for z in range(grid_z):
            at = pl.ds(pl.multiple_of(y * share + z * pair, pair), pair)
            both = jnp.concatenate(
                [
                    rows[(y * grid_core + core) * grid_x + x, z].astype(jnp.float32)
                    for core in range(grid_core)
                ],
                axis=0,
            )
            total = total + both * both
            blocks[x][at, :] = both.astype(jnp.bfloat16)
        return total

    def mix(x, y):
        to = pl.ds(pl.multiple_of(y * share, share), share)
        mixed[to, x * share : (x + 1) * share] = jnp.dot(
            left[y], blocks[x][...], preferred_element_type=jnp.float32
        ).astype(mixed.dtype)

    def mix_beside_gather(x, y, total):
        mix(x, y)
        return gather(x + 1, y, total)

    for copy in row_copies:
        copy.wait()
    grad_sum = lax.fori_loop(
        0, grid_y, functools.partial(gather, 0), jnp.zeros((pair, share), jnp.float32)
    )
    for copy in left_copies:
        copy.wait()
    for x in range(grid_x - 1):
        grad_sum = lax.fori_loop(0, grid_y, functools.partial(mix_beside_gather, x), grad_sum)

    def mix_last(y, carry):
        mix(grid_x - 1, y)
        return carry

    lax.fori_loop(0, grid_y, mix_last, 0)
    for copy in right_copies:
        copy.wait()

    def finish(x, total):
        part = jnp.dot(mixed[...], right[x], preferred_element_type=jnp.float32)
        product[x] = part
        return total + jnp.sum(jnp.square(part), axis=0, keepdims=True)

    update_sum = lax.fori_loop(0, grid_x, finish, jnp.zeros((1, share), jnp.float32))
    entries = float(order * order)
    grad_ms = jnp.sum(grad_sum, axis=(0, 1), keepdims=True) / entries
    update_ms = jnp.sum(update_sum, axis=(0, 1), keepdims=True) / entries
    factor = jnp.sqrt(grad_ms + graft_eps) / jnp.sqrt(update_ms + graft_eps)

    def scatter_tile(tile, carry):
        y, z = tile // grid_z, tile % grid_z
        at = pl.ds(pl.multiple_of(tile * pair, pair), pair)
        for x in range(grid_x):
            scaled = (product[x, at, :] * factor).reshape(grid_core, row_local, share)
            for core in range(grid_core):
                staged[(y * grid_core + core) * grid_x + x, z] = scaled[core].astype(out.dtype)
        return carry

    out_copies = []
    for y, span in enumerate(spans):
        lax.fori_loop(y * grid_z, (y + 1) * grid_z, scatter_tile, 0)
        out_copies.append(
            pltpu.make_async_copy(staged.at[span], out.at[span], sems.at[last_sem + y])
        )
        out_copies[-1].start()
    for copy in out_copies:
        copy.wait()


def precondition_slot(here, core, rows, left_root, right_root, pieces):
    slots, order = right_root.shape[:2]
    share = order // grid_x
    hbm_spec = pl.BlockSpec(memory_space=pltpu.HBM)
    return pl.pallas_call(
        slot_kernel,
        out_shape=jax.ShapeDtypeStruct(rows.shape, rows.dtype),
        in_specs=[pl.BlockSpec(memory_space=pltpu.SMEM)] + [hbm_spec] * (3 + len(pieces)),
        out_specs=hbm_spec,
        scratch_shapes=[
            pltpu.VMEM((grid_x, share, order), jnp.bfloat16),
            pltpu.VMEM((grid_x, order, share), jnp.bfloat16),
            pltpu.VMEM(rows.shape, rows.dtype),
            pltpu.VMEM((order, order), jnp.bfloat16),
            pltpu.VMEM((grid_x, order, share), jnp.float32),
            pltpu.VMEM(rows.shape, rows.dtype),
            pltpu.SemaphoreType.DMA((last_sem + 2 * grid_y,)),
        ]
        + [pltpu.VMEM((order, share), jnp.bfloat16)] * grid_x,
        compiler_params=pltpu.CompilerParams(vmem_limit_bytes=60 * 1024 * 1024),
        cost_estimate=pl.CostEstimate(
            flops=4 * order**3, bytes_accessed=8 * order * order, transcendentals=0
        ),
        name="precondition_slot",
    )(
        jnp.stack([here, jnp.minimum(slot_at(here, core), slots - 1)]),
        rows,
        left_root,
        right_root,
        *pieces,
    )


def program(plane_cap, gradients, parameters, left_root, right_root, assignment):
    block_count, row_local, col_local = gradients.shape
    slots_each = left_root.shape[0]
    chunk = (row_local, col_local)
    here, core = lax.axis_index("x"), lax.axis_index("core")
    pieces = factor_pieces(left_root, right_root, here, core)

    owner = assignment // slots_each
    plane = (owner // grid_core) % grid_z
    owner_core = owner % grid_core
    in_plane = ((owner // (grid_z * grid_core)) * grid_core + owner_core) * grid_x + holder_x(
        assignment % slots_each, owner_core
    )
    ids = jnp.arange(block_count, dtype=jnp.int32)
    earlier = (plane[:, None] == plane[None, :]) & (ids[None, :] < ids[:, None])
    rank = jnp.sum(earlier.astype(jnp.int32), axis=1)
    place_of = plane * plane_cap + rank
    my_z = lax.axis_index("z")
    block_at = place(ids, place_of, grid_z * plane_cap)
    mine = plane == my_z
    rank_at = place(rank, jnp.where(mine, in_plane, plane_devices), plane_devices)
    holder_at = place(in_plane, jnp.where(mine, rank, plane_cap), plane_cap)
    plane_rows, z_rows = plane_devices * grid_z, grid_z * plane_cap

    def z_hop(rows):
        rows = rows.reshape((grid_z, plane_cap) + chunk)
        return lax.all_to_all(rows, "z", 0, 0, tiled=True).reshape((z_rows,) + chunk)

    def plane_hop(rows):
        rows = rows.reshape((plane_devices, grid_z) + chunk)
        return lax.all_to_all(rows, plane_axes, 0, 0, tiled=True)

    rows = vmem_call(pick_kernel, [block_at], [gradients], z_rows, "pick_for_z")
    kernel = functools.partial(pick_runs_kernel, (1, plane_cap, grid_z, 1))
    rows = vmem_call(kernel, [rank_at], [z_hop(rows)], plane_rows, "pick_for_plane")
    rows, pieces = lax.optimization_barrier((rows, pieces))
    rows = plane_hop(rows)
    update = precondition_slot(here, core, rows, left_root, right_root, pieces)
    update = plane_hop(update).reshape((plane_rows,) + chunk)
    kernel = functools.partial(pick_runs_kernel, (grid_z, 1, 1, plane_cap))
    update = vmem_call(kernel, [holder_at], [update], z_rows, "pick_back_for_z")
    update = z_hop(update)
    step_rows = vmem_call(pick_kernel, [place_of], [update], block_count, "pick_step_rows")
    new_params = vmem_call(step_kernel, [], [step_rows, parameters], block_count, "step")
    return step_rows, new_params


def per_device(gradients, parameters, left_root, right_root, assignment):
    plane = (assignment // (left_root.shape[0] * grid_core)) % grid_z
    loads = jnp.sum(
        (plane[None, :] == jnp.arange(grid_z, dtype=jnp.int32)[:, None]).astype(jnp.int32), axis=1
    )
    choice = jnp.max(sum((loads > cap).astype(jnp.int32) for cap in plane_capacities[:-1]))
    branches = [functools.partial(program, cap) for cap in plane_capacities]
    return lax.switch(choice, branches, gradients, parameters, left_root, right_root, assignment)


def solution(mesh):
    grid = Mesh(
        mesh.devices.reshape(grid_y, grid_z, grid_core, grid_x), ("y", "z", "core", "x")
    )
    return jax.shard_map(
        per_device,
        mesh=grid,
        in_specs=(
            P(None, fsdp_axes, "x"),
            P(None, fsdp_axes, "x"),
            P(fsdp_axes, "x", None),
            P(fsdp_axes, None, "x"),
            P(),
        ),
        out_specs=(P(None, fsdp_axes, "x"), P(None, fsdp_axes, "x")),
        check_vma=False,
    )
```

```python
import functools
import jax
import jax.numpy as jnp
from jax import lax
from jax.experimental import pallas as pl
from jax.experimental.pallas import tpu as pltpu
from jax.sharding import Mesh, PartitionSpec as P

graft_eps = 1e-06
step_rate = 0.1

grid_y, grid_z, grid_core, grid_x = 4, 16, 2, 4
plane_axes = ("y", "core", "x")
fsdp_axes = ("y", "z", "core")
plane_devices = grid_y * grid_core * grid_x


def z_place(z, core):
    return ((7 + 2 * core) * z) % grid_z


z_groups = [
    [z_place(place, core) * grid_core + core for place in range(grid_z)]
    for core in range(grid_core)
]
plane_capacities = (13, 14, 15, 16, 18, 24)

pick_run = 8


def pick_kernel(index_ref, src_ref, out_ref):
    def some(step, carry):
        first = step * pick_run
        rows = [src_ref[index_ref[first + i]] for i in range(pick_run)]
        for i in range(pick_run):
            out_ref[first + i] = rows[i]
        return carry

    lax.fori_loop(0, out_ref.shape[0] // pick_run, some, 0)


def pick_runs_kernel(strides, z_in_source, index_ref, z_ref, src_ref, out_ref):
    src_run, src_step, out_run, out_step = strides
    z_at = [z_ref[place] for place in range(grid_z)]

    def one(at, carry):
        src_at, out_at = index_ref[at] * src_run, at * out_run
        for place in range(grid_z):
            a, b = (z_at[place], place) if z_in_source else (place, z_at[place])
            out_ref[out_at + b * out_step] = src_ref[src_at + a * src_step]
        return carry

    lax.fori_loop(0, index_ref.shape[0], one, 0)


def step_kernel(step_ref, parameter_ref, new_ref):
    def some(at, carry):
        rows = pl.ds(at * pick_run, pick_run)
        new_ref[rows] = (
            parameter_ref[rows].astype(jnp.float32)
            - step_rate * step_ref[rows].astype(jnp.float32)
        ).astype(new_ref.dtype)
        return carry

    lax.fori_loop(0, new_ref.shape[0] // pick_run, some, 0)


def vmem_call(kernel, index, arrays, count, name):
    vmem_spec = pl.BlockSpec(memory_space=pltpu.VMEM)
    index_specs = [pl.BlockSpec(memory_space=pltpu.SMEM)] * len(index)
    return pl.pallas_call(
        kernel,
        out_shape=jax.ShapeDtypeStruct((count,) + arrays[0].shape[1:], arrays[0].dtype),
        in_specs=index_specs + [vmem_spec] * len(arrays),
        out_specs=vmem_spec,
        compiler_params=pltpu.CompilerParams(vmem_limit_bytes=32 * 1024 * 1024),
        name=name,
    )(*index, *arrays)


def place(values, keys, size):
    hit = jnp.arange(size, dtype=jnp.int32)[:, None] == keys[None, :]
    return jnp.sum(jnp.where(hit, values[None, :], 0), axis=1)


piece_shifts = (2, 3, 1)


def holder_x(slot, core):
    return (slot + 2 + core) % grid_x


def slot_at(x, core):
    return (x + 2 * grid_x - 2 - core) % grid_x


def pack_kernel(slot_ref, left_ref, right_ref, *refs):
    sems, share = refs[-1], left_ref.shape[1]
    copies = []
    for at, out in enumerate(refs[:-1]):
        slot = slot_ref[at]
        copies.append(
            pltpu.make_async_copy(left_ref.at[slot], out.at[:share], sems.at[at * (grid_x + 1)])
        )
        for part in range(grid_x):
            span = pl.ds(part * share, share)
            copies.append(
                pltpu.make_async_copy(
                    right_ref.at[slot, span],
                    out.at[share:, span],
                    sems.at[at * (grid_x + 1) + 1 + part],
                )
            )
    for copy in copies:
        copy.start()
    for copy in copies:
        copy.wait()


def factor_pieces(left_root, right_root, here, core):
    slots, share, order = left_root.shape
    wanted = jnp.stack(
        [jnp.minimum(slot_at(here + shift, core), slots - 1) for shift in piece_shifts]
    )
    hbm_spec = pl.BlockSpec(memory_space=pltpu.HBM)
    packed = pl.pallas_call(
        pack_kernel,
        out_shape=[jax.ShapeDtypeStruct((2 * share, order), left_root.dtype)] * len(piece_shifts),
        in_specs=[pl.BlockSpec(memory_space=pltpu.SMEM), hbm_spec, hbm_spec],
        out_specs=[pl.BlockSpec(memory_space=pltpu.VMEM)] * len(piece_shifts),
        scratch_shapes=[pltpu.SemaphoreType.DMA((len(piece_shifts) * (grid_x + 1),))],
        compiler_params=pltpu.CompilerParams(vmem_limit_bytes=32 * 1024 * 1024),
        name="pack_factors",
    )(wanted, left_root, right_root)
    got = []
    for shift, piece in zip(piece_shifts, packed):
        pairs = [
            (at * grid_x + src, at * grid_x + (src + shift) % grid_x)
            for at in range(grid_core)
            for src in range(grid_x)
            if slot_at((src + shift) % grid_x, at) < slots
        ]
        got.append(lax.ppermute(piece, ("core", "x"), pairs))
    return got


last_sem = 2 + (grid_x - 1) * (grid_x + 1)


def slot_kernel(here_ref, *refs):
    arrived, own_left, own_right = refs[:3]
    pieces = refs[3 : 2 + grid_x]
    out, left, right, rows, block, mixed, product, staged, sems = refs[2 + grid_x :]
    here, slot = here_ref[0], here_ref[1]
    order = block.shape[0]
    share = order // grid_x
    row_local = rows.shape[2]
    pair = grid_core * row_local
    tiles = order // pair
    left_copies = [pltpu.make_async_copy(own_left.at[slot], left.at[here], sems.at[0])]
    right_copies = [pltpu.make_async_copy(own_right.at[slot], right.at[here], sems.at[1])]
    for number, piece in enumerate(pieces):
        at = lax.rem(here - piece_shifts[number] + grid_x, grid_x)
        first = 2 + number * (grid_x + 1)
        left_copies.append(
            pltpu.make_async_copy(piece.at[:share], left.at[at], sems.at[first])
        )
        for part in range(grid_x):
            span = pl.ds(part * share, share)
            right_copies.append(
                pltpu.make_async_copy(
                    piece.at[share:, span], right.at[at, span], sems.at[first + 1 + part]
                )
            )
    spans = [pl.ds(y * grid_core * grid_x, grid_core * grid_x) for y in range(grid_y)]
    row_copies = [
        pltpu.make_async_copy(arrived.at[span], rows.at[span], sems.at[last_sem + grid_y + y])
        for y, span in enumerate(spans)
    ]
    for copy in row_copies + left_copies + right_copies:
        copy.start()

    def gather_tile(tile, total):
        y, z = tile // grid_z, tile % grid_z
        at = pl.ds(pl.multiple_of(tile * pair, pair), pair)
        for x in range(grid_x):
            both = jnp.concatenate(
                [
                    rows[(y * grid_core + core) * grid_x + x, z].astype(jnp.float32)
                    for core in range(grid_core)
                ],
                axis=0,
            )
            total = total + both * both
            block[at, x * share : (x + 1) * share] = both.astype(block.dtype)
        return total

    grad_sum = jnp.zeros((pair, share), jnp.float32)
    for y in range(grid_y):
        row_copies[y].wait()
        grad_sum = lax.fori_loop(
            y * grid_z, (y + 1) * grid_z, gather_tile, grad_sum, unroll=4
        )
    for copy in left_copies:
        copy.wait()

    def mix(tile, carry):
        at = pl.ds(pl.multiple_of(tile * share, share), share)
        mixed[:, at] = jnp.dot(
            left[...].reshape(order, order), block[:, at], preferred_element_type=jnp.float32
        ).astype(mixed.dtype)
        return carry

    lax.fori_loop(0, grid_x, mix, 0)
    for copy in right_copies:
        copy.wait()

    def finish(x, total):
        part = jnp.dot(mixed[...], right[x], preferred_element_type=jnp.float32)
        product[x] = part
        return total + jnp.sum(jnp.square(part), axis=0, keepdims=True)

    update_sum = lax.fori_loop(0, grid_x, finish, jnp.zeros((1, share), jnp.float32))
    entries = float(order * order)
    grad_ms = jnp.sum(grad_sum, axis=(0, 1), keepdims=True) / entries
    update_ms = jnp.sum(update_sum, axis=(0, 1), keepdims=True) / entries
    factor = jnp.sqrt(grad_ms + graft_eps) / jnp.sqrt(update_ms + graft_eps)

    def scatter_tile(tile, carry):
        y, z = tile // grid_z, tile % grid_z
        at = pl.ds(pl.multiple_of(tile * pair, pair), pair)
        for x in range(grid_x):
            scaled = (product[x, at, :] * factor).reshape(grid_core, row_local, share)
            for core in range(grid_core):
                staged[(y * grid_core + core) * grid_x + x, z] = scaled[core].astype(out.dtype)
        return carry

    out_copies = []
    for y, span in enumerate(spans):
        lax.fori_loop(y * grid_z, (y + 1) * grid_z, scatter_tile, 0, unroll=4)
        out_copies.append(
            pltpu.make_async_copy(staged.at[span], out.at[span], sems.at[last_sem + y])
        )
        out_copies[-1].start()
    for copy in out_copies:
        copy.wait()


def precondition_slot(here, core, rows, left_root, right_root, pieces):
    slots, order = right_root.shape[:2]
    share = order // grid_x
    hbm_spec = pl.BlockSpec(memory_space=pltpu.HBM)
    return pl.pallas_call(
        slot_kernel,
        out_shape=jax.ShapeDtypeStruct(rows.shape, rows.dtype),
        in_specs=[pl.BlockSpec(memory_space=pltpu.SMEM)] + [hbm_spec] * (3 + len(pieces)),
        out_specs=hbm_spec,
        scratch_shapes=[
            pltpu.VMEM((grid_x, share, order), jnp.bfloat16),
            pltpu.VMEM((grid_x, order, share), jnp.bfloat16),
            pltpu.VMEM(rows.shape, rows.dtype),
            pltpu.VMEM((order, order), jnp.bfloat16),
            pltpu.VMEM((order, order), jnp.bfloat16),
            pltpu.VMEM((grid_x, order, share), jnp.float32),
            pltpu.VMEM(rows.shape, rows.dtype),
            pltpu.SemaphoreType.DMA((last_sem + 2 * grid_y,)),
        ],
        compiler_params=pltpu.CompilerParams(vmem_limit_bytes=60 * 1024 * 1024),
        cost_estimate=pl.CostEstimate(
            flops=4 * order**3, bytes_accessed=8 * order * order, transcendentals=0
        ),
        name="precondition_slot",
    )(
        jnp.stack([here, jnp.minimum(slot_at(here, core), slots - 1)]),
        rows,
        left_root,
        right_root,
        *pieces,
    )


def program(plane_cap, gradients, parameters, left_root, right_root, assignment):
    block_count, row_local, col_local = gradients.shape
    slots_each = left_root.shape[0]
    chunk = (row_local, col_local)
    here, core = lax.axis_index("x"), lax.axis_index("core")
    pieces = factor_pieces(left_root, right_root, here, core)

    owner = assignment // slots_each
    plane = (owner // grid_core) % grid_z
    owner_core = owner % grid_core
    in_plane = ((owner // (grid_z * grid_core)) * grid_core + owner_core) * grid_x + holder_x(
        assignment % slots_each, owner_core
    )
    ids = jnp.arange(block_count, dtype=jnp.int32)
    earlier = (plane[:, None] == plane[None, :]) & (ids[None, :] < ids[:, None])
    rank = jnp.sum(earlier.astype(jnp.int32), axis=1)
    place_of = z_place(plane, core) * plane_cap + rank
    my_z = lax.axis_index("z")
    z_at = z_place(jnp.arange(grid_z, dtype=jnp.int32), core)
    block_at = place(ids, place_of, grid_z * plane_cap)
    mine = plane == my_z
    rank_at = place(rank, jnp.where(mine, in_plane, plane_devices), plane_devices)
    holder_at = place(in_plane, jnp.where(mine, rank, plane_cap), plane_cap)
    plane_rows, z_rows = plane_devices * grid_z, grid_z * plane_cap

    def z_hop(rows):
        rows = rows.reshape((grid_z, plane_cap) + chunk)
        rows = lax.all_to_all(
            rows, ("z", "core"), 0, 0, axis_index_groups=z_groups, tiled=True
        )
        return rows.reshape((z_rows,) + chunk)

    def plane_hop(rows):
        rows = rows.reshape((plane_devices, grid_z) + chunk)
        return lax.all_to_all(rows, plane_axes, 0, 0, tiled=True)

    rows = vmem_call(pick_kernel, [block_at], [gradients], z_rows, "pick_for_z")
    kernel = functools.partial(pick_runs_kernel, (1, plane_cap, grid_z, 1), False)
    rows = vmem_call(kernel, [rank_at, z_at], [z_hop(rows)], plane_rows, "pick_for_plane")
    rows, pieces = lax.optimization_barrier((rows, pieces))
    rows = plane_hop(rows)
    update = precondition_slot(here, core, rows, left_root, right_root, pieces)
    update = plane_hop(update).reshape((plane_rows,) + chunk)
    kernel = functools.partial(pick_runs_kernel, (grid_z, 1, 1, plane_cap), True)
    update = vmem_call(kernel, [holder_at, z_at], [update], z_rows, "pick_back_for_z")
    update = z_hop(update)
    step_rows = vmem_call(pick_kernel, [place_of], [update], block_count, "pick_step_rows")
    new_params = vmem_call(step_kernel, [], [step_rows, parameters], block_count, "step")
    return step_rows, new_params


def per_device(gradients, parameters, left_root, right_root, assignment):
    plane = (assignment // (left_root.shape[0] * grid_core)) % grid_z
    loads = jnp.sum(
        (plane[None, :] == jnp.arange(grid_z, dtype=jnp.int32)[:, None]).astype(jnp.int32), axis=1
    )
    choice = jnp.max(sum((loads > cap).astype(jnp.int32) for cap in plane_capacities[:-1]))
    branches = [functools.partial(program, cap) for cap in plane_capacities]
    return lax.switch(choice, branches, gradients, parameters, left_root, right_root, assignment)


def solution(mesh):
    grid = Mesh(
        mesh.devices.reshape(grid_y, grid_z, grid_core, grid_x), ("y", "z", "core", "x")
    )
    return jax.shard_map(
        per_device,
        mesh=grid,
        in_specs=(
            P(None, fsdp_axes, "x"),
            P(None, fsdp_axes, "x"),
            P(fsdp_axes, "x", None),
            P(fsdp_axes, None, "x"),
            P(),
        ),
        out_specs=(P(None, fsdp_axes, "x"), P(None, fsdp_axes, "x")),
        check_vma=False,
    )
```

```python
import functools
import jax
import jax.numpy as jnp
from jax import lax
from jax.experimental import pallas as pl
from jax.experimental.pallas import tpu as pltpu
from jax.sharding import Mesh, PartitionSpec as P

graft_eps = 1e-06
step_rate = 0.1

grid_y, grid_z, grid_core, grid_x = 4, 16, 2, 4
plane_axes = ("y", "core", "x")
fsdp_axes = ("y", "z", "core")
plane_devices = grid_y * grid_core * grid_x
plane_capacities = (13, 14, 15, 16, 18, 24)

pick_run = 8


def pick_kernel(index_ref, src_ref, out_ref):
    def some(step, carry):
        first = step * pick_run
        rows = [src_ref[index_ref[first + i]] for i in range(pick_run)]
        for i in range(pick_run):
            out_ref[first + i] = rows[i]
        return carry

    lax.fori_loop(0, out_ref.shape[0] // pick_run, some, 0)


def pick_runs_kernel(strides, index_ref, src_ref, out_ref):
    src_run, src_step, out_run, out_step = strides

    def one(at, carry):
        src_at, out_at = index_ref[at] * src_run, at * out_run
        for z in range(grid_z):
            out_ref[out_at + z * out_step] = src_ref[src_at + z * src_step]
        return carry

    lax.fori_loop(0, index_ref.shape[0], one, 0)


def step_kernel(step_ref, parameter_ref, new_ref):
    def some(at, carry):
        rows = pl.ds(at * pick_run, pick_run)
        new_ref[rows] = (
            parameter_ref[rows].astype(jnp.float32)
            - step_rate * step_ref[rows].astype(jnp.float32)
        ).astype(new_ref.dtype)
        return carry

    lax.fori_loop(0, new_ref.shape[0] // pick_run, some, 0)


def vmem_call(kernel, index, arrays, count, name):
    vmem_spec = pl.BlockSpec(memory_space=pltpu.VMEM)
    index_specs = [pl.BlockSpec(memory_space=pltpu.SMEM)] * len(index)
    return pl.pallas_call(
        kernel,
        out_shape=jax.ShapeDtypeStruct((count,) + arrays[0].shape[1:], arrays[0].dtype),
        in_specs=index_specs + [vmem_spec] * len(arrays),
        out_specs=vmem_spec,
        compiler_params=pltpu.CompilerParams(vmem_limit_bytes=32 * 1024 * 1024),
        name=name,
    )(*index, *arrays)


def place(values, keys, size):
    hit = jnp.arange(size, dtype=jnp.int32)[:, None] == keys[None, :]
    return jnp.sum(jnp.where(hit, values[None, :], 0), axis=1)


piece_shifts = (2, 3, 1)


def holder_x(slot, core):
    return (slot + 2 + core) % grid_x


def slot_at(x, core):
    return (x + 2 * grid_x - 2 - core) % grid_x


def pack_kernel(slot_ref, left_ref, right_ref, out, sems):
    slot, share = slot_ref[0], left_ref.shape[1]
    copies = [pltpu.make_async_copy(left_ref.at[slot], out.at[:share], sems.at[grid_x])]
    for part in range(grid_x):
        span = pl.ds(part * share, share)
        copies.append(
            pltpu.make_async_copy(right_ref.at[slot, span], out.at[share:, span], sems.at[part])
        )
    for copy in copies:
        copy.start()
    for copy in copies:
        copy.wait()


def factor_pieces(left_root, right_root, here, core):
    slots, share, order = left_root.shape
    hbm_spec = pl.BlockSpec(memory_space=pltpu.HBM)
    got = []
    for shift in piece_shifts:
        piece = pl.pallas_call(
            pack_kernel,
            out_shape=jax.ShapeDtypeStruct((2 * share, order), left_root.dtype),
            in_specs=[pl.BlockSpec(memory_space=pltpu.SMEM), hbm_spec, hbm_spec],
            out_specs=pl.BlockSpec(memory_space=pltpu.VMEM),
            scratch_shapes=[pltpu.SemaphoreType.DMA((grid_x + 1,))],
            compiler_params=pltpu.CompilerParams(vmem_limit_bytes=32 * 1024 * 1024),
            name="pack_factors",
        )(jnp.minimum(slot_at(here + shift, core), slots - 1).reshape(1), left_root, right_root)
        pairs = [
            (at * grid_x + src, at * grid_x + (src + shift) % grid_x)
            for at in range(grid_core)
            for src in range(grid_x)
            if slot_at((src + shift) % grid_x, at) < slots
        ]
        got.append(lax.ppermute(piece, ("core", "x"), pairs))
    return got


last_sem = 2 + (grid_x - 1) * (grid_x + 1)


def slot_kernel(here_ref, *refs):
    arrived, own_left, own_right = refs[:3]
    pieces = refs[3 : 2 + grid_x]
    out, left, right, rows, block, mixed, product, staged, sems = refs[2 + grid_x :]
    here, slot = here_ref[0], here_ref[1]
    order = block.shape[0]
    share = order // grid_x
    row_local = rows.shape[2]
    pair = grid_core * row_local
    tiles = order // pair
    left_copies = [pltpu.make_async_copy(own_left.at[slot], left.at[here], sems.at[0])]
    right_copies = [pltpu.make_async_copy(own_right.at[slot], right.at[here], sems.at[1])]
    for number, piece in enumerate(pieces):
        at = lax.rem(here - piece_shifts[number] + grid_x, grid_x)
        first = 2 + number * (grid_x + 1)
        left_copies.append(
            pltpu.make_async_copy(piece.at[:share], left.at[at], sems.at[first])
        )
        for part in range(grid_x):
            span = pl.ds(part * share, share)
            right_copies.append(
                pltpu.make_async_copy(
                    piece.at[share:, span], right.at[at, span], sems.at[first + 1 + part]
                )
            )
    spans = [pl.ds(y * grid_core * grid_x, grid_core * grid_x) for y in range(grid_y)]
    row_copies = [
        pltpu.make_async_copy(arrived.at[span], rows.at[span], sems.at[last_sem + grid_y + y])
        for y, span in enumerate(spans)
    ]
    for copy in row_copies + left_copies + right_copies:
        copy.start()

    def gather_tile(tile, total):
        y, z = tile // grid_z, tile % grid_z
        at = pl.ds(pl.multiple_of(tile * pair, pair), pair)
        for x in range(grid_x):
            both = jnp.concatenate(
                [
                    rows[(y * grid_core + core) * grid_x + x, z].astype(jnp.float32)
                    for core in range(grid_core)
                ],
                axis=0,
            )
            total = total + both * both
            block[at, x * share : (x + 1) * share] = both.astype(block.dtype)
        return total

    grad_sum = jnp.zeros((pair, share), jnp.float32)
    for y in range(grid_y):
        row_copies[y].wait()
        grad_sum = lax.fori_loop(y * grid_z, (y + 1) * grid_z, gather_tile, grad_sum)
    for copy in left_copies:
        copy.wait()

    def mix(tile, carry):
        at = pl.ds(pl.multiple_of(tile * share, share), share)
        mixed[:, at] = jnp.dot(
            left[...].reshape(order, order), block[:, at], preferred_element_type=jnp.float32
        ).astype(mixed.dtype)
        return carry

    lax.fori_loop(0, grid_x, mix, 0)
    for copy in right_copies:
        copy.wait()

    def finish(x, total):
        part = jnp.dot(mixed[...], right[x], preferred_element_type=jnp.float32)
        product[x] = part
        return total + jnp.sum(jnp.square(part), axis=0, keepdims=True)

    update_sum = lax.fori_loop(0, grid_x, finish, jnp.zeros((1, share), jnp.float32))
    entries = float(order * order)
    grad_ms = jnp.sum(grad_sum, axis=(0, 1), keepdims=True) / entries
    update_ms = jnp.sum(update_sum, axis=(0, 1), keepdims=True) / entries
    factor = jnp.sqrt(grad_ms + graft_eps) / jnp.sqrt(update_ms + graft_eps)

    def scatter_tile(tile, carry):
        y, z = tile // grid_z, tile % grid_z
        at = pl.ds(pl.multiple_of(tile * pair, pair), pair)
        for x in range(grid_x):
            scaled = (product[x, at, :] * factor).reshape(grid_core, row_local, share)
            for core in range(grid_core):
                staged[(y * grid_core + core) * grid_x + x, z] = scaled[core].astype(out.dtype)
        return carry

    out_copies = []
    for y, span in enumerate(spans):
        lax.fori_loop(y * grid_z, (y + 1) * grid_z, scatter_tile, 0)
        out_copies.append(
            pltpu.make_async_copy(staged.at[span], out.at[span], sems.at[last_sem + y])
        )
        out_copies[-1].start()
    for copy in out_copies:
        copy.wait()


def precondition_slot(here, core, rows, left_root, right_root, pieces):
    slots, order = right_root.shape[:2]
    share = order // grid_x
    hbm_spec = pl.BlockSpec(memory_space=pltpu.HBM)
    return pl.pallas_call(
        slot_kernel,
        out_shape=jax.ShapeDtypeStruct(rows.shape, rows.dtype),
        in_specs=[pl.BlockSpec(memory_space=pltpu.SMEM)] + [hbm_spec] * (3 + len(pieces)),
        out_specs=hbm_spec,
        scratch_shapes=[
            pltpu.VMEM((grid_x, share, order), jnp.bfloat16),
            pltpu.VMEM((grid_x, order, share), jnp.bfloat16),
            pltpu.VMEM(rows.shape, rows.dtype),
            pltpu.VMEM((order, order), jnp.bfloat16),
            pltpu.VMEM((order, order), jnp.bfloat16),
            pltpu.VMEM((grid_x, order, share), jnp.float32),
            pltpu.VMEM(rows.shape, rows.dtype),
            pltpu.SemaphoreType.DMA((last_sem + 2 * grid_y,)),
        ],
        compiler_params=pltpu.CompilerParams(vmem_limit_bytes=60 * 1024 * 1024),
        cost_estimate=pl.CostEstimate(
            flops=4 * order**3, bytes_accessed=8 * order * order, transcendentals=0
        ),
        name="precondition_slot",
    )(
        jnp.stack([here, jnp.minimum(slot_at(here, core), slots - 1)]),
        rows,
        left_root,
        right_root,
        *pieces,
    )


def program(plane_cap, gradients, parameters, left_root, right_root, assignment):
    block_count, row_local, col_local = gradients.shape
    slots_each = left_root.shape[0]
    chunk = (row_local, col_local)
    here, core = lax.axis_index("x"), lax.axis_index("core")
    pieces = factor_pieces(left_root, right_root, here, core)

    owner = assignment // slots_each
    plane = (owner // grid_core) % grid_z
    owner_core = owner % grid_core
    in_plane = ((owner // (grid_z * grid_core)) * grid_core + owner_core) * grid_x + holder_x(
        assignment % slots_each, owner_core
    )
    ids = jnp.arange(block_count, dtype=jnp.int32)
    earlier = (plane[:, None] == plane[None, :]) & (ids[None, :] < ids[:, None])
    rank = jnp.sum(earlier.astype(jnp.int32), axis=1)
    place_of = plane * plane_cap + rank
    my_z = lax.axis_index("z")
    block_at = place(ids, place_of, grid_z * plane_cap)
    mine = plane == my_z
    rank_at = place(rank, jnp.where(mine, in_plane, plane_devices), plane_devices)
    holder_at = place(in_plane, jnp.where(mine, rank, plane_cap), plane_cap)
    plane_rows, z_rows = plane_devices * grid_z, grid_z * plane_cap

    def z_hop(rows):
        rows = rows.reshape((grid_z, plane_cap) + chunk)
        return lax.all_to_all(rows, "z", 0, 0, tiled=True).reshape((z_rows,) + chunk)

    def plane_hop(rows):
        rows = rows.reshape((plane_devices, grid_z) + chunk)
        return lax.all_to_all(rows, plane_axes, 0, 0, tiled=True)

    rows = vmem_call(pick_kernel, [block_at], [gradients], z_rows, "pick_for_z")
    kernel = functools.partial(pick_runs_kernel, (1, plane_cap, grid_z, 1))
    rows = vmem_call(kernel, [rank_at], [z_hop(rows)], plane_rows, "pick_for_plane")
    rows, pieces = lax.optimization_barrier((rows, pieces))
    rows = plane_hop(rows)
    update = precondition_slot(here, core, rows, left_root, right_root, pieces)
    update = plane_hop(update).reshape((plane_rows,) + chunk)
    kernel = functools.partial(pick_runs_kernel, (grid_z, 1, 1, plane_cap))
    update = vmem_call(kernel, [holder_at], [update], z_rows, "pick_back_for_z")
    update = z_hop(update)
    step_rows = vmem_call(pick_kernel, [place_of], [update], block_count, "pick_step_rows")
    new_params = vmem_call(step_kernel, [], [step_rows, parameters], block_count, "step")
    return step_rows, new_params


def per_device(gradients, parameters, left_root, right_root, assignment):
    plane = (assignment // (left_root.shape[0] * grid_core)) % grid_z
    loads = jnp.sum(
        (plane[None, :] == jnp.arange(grid_z, dtype=jnp.int32)[:, None]).astype(jnp.int32), axis=1
    )
    choice = jnp.max(sum((loads > cap).astype(jnp.int32) for cap in plane_capacities[:-1]))
    branches = [functools.partial(program, cap) for cap in plane_capacities]
    return lax.switch(choice, branches, gradients, parameters, left_root, right_root, assignment)


def solution(mesh):
    grid = Mesh(
        mesh.devices.reshape(grid_y, grid_z, grid_core, grid_x), ("y", "z", "core", "x")
    )
    return jax.shard_map(
        per_device,
        mesh=grid,
        in_specs=(
            P(None, fsdp_axes, "x"),
            P(None, fsdp_axes, "x"),
            P(fsdp_axes, "x", None),
            P(fsdp_axes, None, "x"),
            P(),
        ),
        out_specs=(P(None, fsdp_axes, "x"), P(None, fsdp_axes, "x")),
        check_vma=False,
    )
```

```python
import functools
import jax
import jax.numpy as jnp
from jax import lax
from jax.experimental import pallas as pl
from jax.experimental.pallas import tpu as pltpu
from jax.sharding import Mesh, PartitionSpec as P

graft_eps = 1e-06
step_rate = 0.1

grid_y, grid_z, grid_core, grid_x = 4, 16, 2, 4
plane_axes = ("y", "core", "x")
fsdp_axes = ("y", "z", "core")
plane_devices = grid_y * grid_core * grid_x
plane_capacities = (13, 14, 15, 16, 18, 24)

pick_run = 8


def pick_kernel(index_ref, src_ref, out_ref):
    def some(step, carry):
        first = step * pick_run
        rows = [src_ref[index_ref[first + i]] for i in range(pick_run)]
        for i in range(pick_run):
            out_ref[first + i] = rows[i]
        return carry

    lax.fori_loop(0, out_ref.shape[0] // pick_run, some, 0)


def place_kernel(index_ref, src_ref, out_ref):
    def some(step, carry):
        first = step * pick_run
        rows = [src_ref[first + i] for i in range(pick_run)]
        for i in range(pick_run):
            out_ref[index_ref[first + i]] = rows[i]
        return carry

    lax.fori_loop(0, src_ref.shape[0] // pick_run, some, 0)


def pick_runs_kernel(strides, index_ref, src_ref, out_ref):
    src_run, src_step, out_run, out_step = strides

    def one(at, carry):
        src_at, out_at = index_ref[at] * src_run, at * out_run
        for z in range(grid_z):
            out_ref[out_at + z * out_step] = src_ref[src_at + z * src_step]
        return carry

    lax.fori_loop(0, index_ref.shape[0], one, 0)


def step_kernel(step_ref, parameter_ref, new_ref):
    def some(at, carry):
        rows = pl.ds(at * pick_run, pick_run)
        new_ref[rows] = (
            parameter_ref[rows].astype(jnp.float32)
            - step_rate * step_ref[rows].astype(jnp.float32)
        ).astype(new_ref.dtype)
        return carry

    lax.fori_loop(0, new_ref.shape[0] // pick_run, some, 0)


def vmem_call(kernel, index, arrays, count, name):
    vmem_spec = pl.BlockSpec(memory_space=pltpu.VMEM)
    index_specs = [pl.BlockSpec(memory_space=pltpu.SMEM)] * len(index)
    return pl.pallas_call(
        kernel,
        out_shape=jax.ShapeDtypeStruct((count,) + arrays[0].shape[1:], arrays[0].dtype),
        in_specs=index_specs + [vmem_spec] * len(arrays),
        out_specs=vmem_spec,
        compiler_params=pltpu.CompilerParams(vmem_limit_bytes=32 * 1024 * 1024),
        name=name,
    )(*index, *arrays)


def place(values, keys, size):
    hit = jnp.arange(size, dtype=jnp.int32)[:, None] == keys[None, :]
    return jnp.sum(jnp.where(hit, values[None, :], 0), axis=1)


piece_shifts = (2, 3, 1)


def holder_x(slot, core):
    return (slot + 2 + core) % grid_x


def slot_at(x, core):
    return (x + 2 * grid_x - 2 - core) % grid_x


def pack_kernel(slot_ref, left_ref, right_ref, out, sems):
    slot, share = slot_ref[0], left_ref.shape[1]
    copies = [pltpu.make_async_copy(left_ref.at[slot], out.at[:share], sems.at[grid_x])]
    for part in range(grid_x):
        span = pl.ds(part * share, share)
        copies.append(
            pltpu.make_async_copy(right_ref.at[slot, span], out.at[share:, span], sems.at[part])
        )
    for copy in copies:
        copy.start()
    for copy in copies:
        copy.wait()


def factor_pieces(left_root, right_root, here, core):
    slots, share, order = left_root.shape
    hbm_spec = pl.BlockSpec(memory_space=pltpu.HBM)
    got = []
    for shift in piece_shifts:
        piece = pl.pallas_call(
            pack_kernel,
            out_shape=jax.ShapeDtypeStruct((2 * share, order), left_root.dtype),
            in_specs=[pl.BlockSpec(memory_space=pltpu.SMEM), hbm_spec, hbm_spec],
            out_specs=pl.BlockSpec(memory_space=pltpu.VMEM),
            scratch_shapes=[pltpu.SemaphoreType.DMA((grid_x + 1,))],
            compiler_params=pltpu.CompilerParams(vmem_limit_bytes=32 * 1024 * 1024),
            name="pack_factors",
        )(jnp.minimum(slot_at(here + shift, core), slots - 1).reshape(1), left_root, right_root)
        pairs = [
            (at * grid_x + src, at * grid_x + (src + shift) % grid_x)
            for at in range(grid_core)
            for src in range(grid_x)
            if slot_at((src + shift) % grid_x, at) < slots
        ]
        got.append(lax.ppermute(piece, ("core", "x"), pairs))
    return got


last_sem = 2 + (grid_x - 1) * (grid_x + 1)


def slot_kernel(here_ref, *refs):
    arrived, own_left, own_right = refs[:3]
    pieces = refs[3 : 2 + grid_x]
    out, left, right, rows, block, mixed, product, staged, sems = refs[2 + grid_x :]
    here, slot = here_ref[0], here_ref[1]
    order = block.shape[0]
    share = order // grid_x
    row_local = rows.shape[2]
    pair = grid_core * row_local
    tiles = order // pair
    left_copies = [pltpu.make_async_copy(own_left.at[slot], left.at[here], sems.at[0])]
    right_copies = [pltpu.make_async_copy(own_right.at[slot], right.at[here], sems.at[1])]
    for number, piece in enumerate(pieces):
        at = lax.rem(here - piece_shifts[number] + grid_x, grid_x)
        first = 2 + number * (grid_x + 1)
        left_copies.append(
            pltpu.make_async_copy(piece.at[:share], left.at[at], sems.at[first])
        )
        for part in range(grid_x):
            span = pl.ds(part * share, share)
            right_copies.append(
                pltpu.make_async_copy(
                    piece.at[share:, span], right.at[at, span], sems.at[first + 1 + part]
                )
            )
    spans = [pl.ds(y * grid_core * grid_x, grid_core * grid_x) for y in range(grid_y)]
    row_copies = [
        pltpu.make_async_copy(arrived.at[span], rows.at[span], sems.at[last_sem + grid_y + y])
        for y, span in enumerate(spans)
    ]
    for copy in row_copies + left_copies + right_copies:
        copy.start()

    def gather_tile(tile, total):
        y, z = tile // grid_z, tile % grid_z
        at = pl.ds(pl.multiple_of(tile * pair, pair), pair)
        for x in range(grid_x):
            both = jnp.concatenate(
                [
                    rows[(y * grid_core + core) * grid_x + x, z].astype(jnp.float32)
                    for core in range(grid_core)
                ],
                axis=0,
            )
            total = total + both * both
            block[at, x * share : (x + 1) * share] = both.astype(block.dtype)
        return total

    grad_sum = jnp.zeros((pair, share), jnp.float32)
    for y in range(grid_y):
        row_copies[y].wait()
        grad_sum = lax.fori_loop(y * grid_z, (y + 1) * grid_z, gather_tile, grad_sum)
    for copy in left_copies:
        copy.wait()

    def mix(tile, carry):
        at = pl.ds(pl.multiple_of(tile * share, share), share)
        mixed[:, at] = jnp.dot(
            left[...].reshape(order, order), block[:, at], preferred_element_type=jnp.float32
        ).astype(mixed.dtype)
        return carry

    lax.fori_loop(0, grid_x, mix, 0)
    for copy in right_copies:
        copy.wait()

    def finish(x, total):
        part = jnp.dot(mixed[...], right[x], preferred_element_type=jnp.float32)
        product[x] = part
        return total + jnp.sum(jnp.square(part), axis=0, keepdims=True)

    update_sum = lax.fori_loop(0, grid_x, finish, jnp.zeros((1, share), jnp.float32))
    entries = float(order * order)
    grad_ms = jnp.sum(grad_sum, axis=(0, 1), keepdims=True) / entries
    update_ms = jnp.sum(update_sum, axis=(0, 1), keepdims=True) / entries
    factor = jnp.sqrt(grad_ms + graft_eps) / jnp.sqrt(update_ms + graft_eps)

    def scatter_tile(tile, carry):
        y, z = tile // grid_z, tile % grid_z
        at = pl.ds(pl.multiple_of(tile * pair, pair), pair)
        for x in range(grid_x):
            scaled = (product[x, at, :] * factor).reshape(grid_core, row_local, share)
            for core in range(grid_core):
                staged[(y * grid_core + core) * grid_x + x, z] = scaled[core].astype(out.dtype)
        return carry

    out_copies = []
    for y, span in enumerate(spans):
        lax.fori_loop(y * grid_z, (y + 1) * grid_z, scatter_tile, 0)
        out_copies.append(
            pltpu.make_async_copy(staged.at[span], out.at[span], sems.at[last_sem + y])
        )
        out_copies[-1].start()
    for copy in out_copies:
        copy.wait()


def precondition_slot(here, core, rows, left_root, right_root, pieces):
    slots, order = right_root.shape[:2]
    share = order // grid_x
    hbm_spec = pl.BlockSpec(memory_space=pltpu.HBM)
    return pl.pallas_call(
        slot_kernel,
        out_shape=jax.ShapeDtypeStruct(rows.shape, rows.dtype),
        in_specs=[pl.BlockSpec(memory_space=pltpu.SMEM)] + [hbm_spec] * (3 + len(pieces)),
        out_specs=hbm_spec,
        scratch_shapes=[
            pltpu.VMEM((grid_x, share, order), jnp.bfloat16),
            pltpu.VMEM((grid_x, order, share), jnp.bfloat16),
            pltpu.VMEM(rows.shape, rows.dtype),
            pltpu.VMEM((order, order), jnp.bfloat16),
            pltpu.VMEM((order, order), jnp.bfloat16),
            pltpu.VMEM((grid_x, order, share), jnp.float32),
            pltpu.VMEM(rows.shape, rows.dtype),
            pltpu.SemaphoreType.DMA((last_sem + 2 * grid_y,)),
        ],
        compiler_params=pltpu.CompilerParams(vmem_limit_bytes=60 * 1024 * 1024),
        cost_estimate=pl.CostEstimate(
            flops=4 * order**3, bytes_accessed=8 * order * order, transcendentals=0
        ),
        name="precondition_slot",
    )(
        jnp.stack([here, jnp.minimum(slot_at(here, core), slots - 1)]),
        rows,
        left_root,
        right_root,
        *pieces,
    )


def program(plane_cap, gradients, parameters, left_root, right_root, assignment):
    block_count, row_local, col_local = gradients.shape
    slots_each = left_root.shape[0]
    chunk = (row_local, col_local)
    here, core = lax.axis_index("x"), lax.axis_index("core")
    pieces = factor_pieces(left_root, right_root, here, core)

    owner = assignment // slots_each
    plane = (owner // grid_core) % grid_z
    owner_core = owner % grid_core
    in_plane = ((owner // (grid_z * grid_core)) * grid_core + owner_core) * grid_x + holder_x(
        assignment % slots_each, owner_core
    )
    ids = jnp.arange(block_count, dtype=jnp.int32)
    earlier = (plane[:, None] == plane[None, :]) & (ids[None, :] < ids[:, None])
    rank = jnp.sum(earlier.astype(jnp.int32), axis=1)
    place_of = plane * plane_cap + rank
    my_z = lax.axis_index("z")
    mine = plane == my_z
    rank_at = place(rank, jnp.where(mine, in_plane, plane_devices), plane_devices)
    holder_at = place(in_plane, jnp.where(mine, rank, plane_cap), plane_cap)
    plane_rows, z_rows = plane_devices * grid_z, grid_z * plane_cap

    def z_hop(rows):
        rows = rows.reshape((grid_z, plane_cap) + chunk)
        return lax.all_to_all(rows, "z", 0, 0, tiled=True).reshape((z_rows,) + chunk)

    def plane_hop(rows):
        rows = rows.reshape((plane_devices, grid_z) + chunk)
        return lax.all_to_all(rows, plane_axes, 0, 0, tiled=True)

    rows = vmem_call(place_kernel, [place_of], [gradients], z_rows, "place_for_z")
    kernel = functools.partial(pick_runs_kernel, (1, plane_cap, grid_z, 1))
    rows = vmem_call(kernel, [rank_at], [z_hop(rows)], plane_rows, "pick_for_plane")
    rows, pieces = lax.optimization_barrier((rows, pieces))
    rows = plane_hop(rows)
    update = precondition_slot(here, core, rows, left_root, right_root, pieces)
    update = plane_hop(update).reshape((plane_rows,) + chunk)
    kernel = functools.partial(pick_runs_kernel, (grid_z, 1, 1, plane_cap))
    update = vmem_call(kernel, [holder_at], [update], z_rows, "pick_back_for_z")
    update = z_hop(update)
    step_rows = vmem_call(pick_kernel, [place_of], [update], block_count, "pick_step_rows")
    new_params = vmem_call(step_kernel, [], [step_rows, parameters], block_count, "step")
    return step_rows, new_params


def per_device(gradients, parameters, left_root, right_root, assignment):
    plane = (assignment // (left_root.shape[0] * grid_core)) % grid_z
    loads = jnp.sum(
        (plane[None, :] == jnp.arange(grid_z, dtype=jnp.int32)[:, None]).astype(jnp.int32), axis=1
    )
    choice = jnp.max(sum((loads > cap).astype(jnp.int32) for cap in plane_capacities[:-1]))
    branches = [functools.partial(program, cap) for cap in plane_capacities]
    return lax.switch(choice, branches, gradients, parameters, left_root, right_root, assignment)


def solution(mesh):
    grid = Mesh(
        mesh.devices.reshape(grid_y, grid_z, grid_core, grid_x), ("y", "z", "core", "x")
    )
    return jax.shard_map(
        per_device,
        mesh=grid,
        in_specs=(
            P(None, fsdp_axes, "x"),
            P(None, fsdp_axes, "x"),
            P(fsdp_axes, "x", None),
            P(fsdp_axes, None, "x"),
            P(),
        ),
        out_specs=(P(None, fsdp_axes, "x"), P(None, fsdp_axes, "x")),
        check_vma=False,
    )
```
